32 devices in a mesh: src: 8 (over z, core), tgt: 4 (over y, x).
Axes of the slice: x: 2, y: 2, z: 4, core: 2. Of those that a mesh axis runs over, the one named last changes fastest.
Arguments:
- source_field: bfloat16 [1024, 256, 256], P(None, ('src', 'tgt')), may hold values from -6 to 6
- self_weight: bfloat16 [4, 256, 256, 256], P(None, ('src', 'tgt')), may hold values from -0.25 to 0.25
- cross_weight: bfloat16 [4, 256, 256, 256], P(None, ('src', 'tgt')), may hold values from -0.25 to 0.25
- level_bias: float32 [4, 256, 256], P(None, ('src', 'tgt')), may hold values from -3 to 3
- switch_weight: bfloat16 [256, 256, 256], P(('src', 'tgt')), may hold values from -0.375 to 0.375
- switch_bias: float32 [256, 256], P(('src', 'tgt')), may hold values from -3 to 3
Outputs:
- target_field: bfloat16 [1024, 256, 256], P(None, ('src', 'tgt'))
The draws below stay inside these ranges and needn't reach their ends.
All inputs are finite; a program needn't handle non-finite values.
Results may differ from the reference program's by a relative error of at most 0.0057.
Values may be sent and summed in bfloat16 or wider, within the bound.
No kernel may reach another device: no remote copies, remote signals or barrier semaphores. Data moves between devices by JAX's collectives and lax.ppermute only.
A program may use at most 64 MiB of HBM per device.

```python
import jax
import jax.numpy as jnp
from jax import lax

W = 256
BLK_DEV = 8
SHOTS = 1024
LEVELS = 4
NB = 256
STRIDE = 32
GROUP = 4
PIECE = 64


def level_of(stream_key, shape, shards, least, high):
    level, own = 1.0, jax.random.fold_in(stream_key, 6)
    for dim, shards_of in shards:
        heights = jnp.exp(jax.random.uniform(jax.random.fold_in(own, dim), (shards_of,), jnp.float32, least / len(shards), high / len(shards)))
        level = level * jnp.repeat(heights, shape[dim] // shards_of).reshape([-1 if axis == dim else 1 for axis in range(len(shape))])
    return level


def noise(rng, dims, spread, limit, shards=(), dtype=jnp.bfloat16):
    entries = spread * jax.random.normal(rng, dims, jnp.float32)
    if shards:
        entries = entries * level_of(rng, dims, shards, -0.22, 0.18)
    return jnp.clip(entries, -limit, limit).astype(dtype)


def setup_inputs(seed: int = 0) -> dict:
    splits = jax.random.split(jax.random.key(seed), 7)
    source_field = noise(splits[0], (SHOTS, NB, W), 1.0, 6.0, ((1, 32),))
    self_weight = noise(splits[1], (LEVELS, NB, W, W), (2 * W) ** -0.5, 0.25, ((1, 32),))
    cross_weight = noise(splits[2], (LEVELS, NB, W, W), (2 * W) ** -0.5, 0.25, ((1, 32),))
    level_bias = noise(splits[3], (LEVELS, NB, W), 0.5, 3.0, ((1, 32),), jnp.float32)
    switch_weight = noise(splits[4], (NB, W, W), W ** -0.5, 0.375, ((0, 32),))
    switch_bias = noise(splits[5], (NB, W), 0.5, 3.0, ((0, 32),), jnp.float32)
    return dict(source_field=source_field, self_weight=self_weight, cross_weight=cross_weight, level_bias=level_bias, switch_weight=switch_weight, switch_bias=switch_bias)


def partner(values, dist):
    shots, blocks, width = values.shape
    grouped = values.reshape(shots, blocks // (2 * dist), 2, dist, width)
    return grouped[:, :, ::-1].reshape(shots, blocks, width)


def level_step(field, self_w, cross_w, bias, dist):
    inputs = field.astype(jnp.float32)
    own_part = jnp.einsum("sbi,bio->sbo", inputs, self_w.astype(jnp.float32), precision=lax.Precision.HIGHEST)
    term = jnp.einsum("sbi,bio->sbo", inputs, cross_w.astype(jnp.float32), precision=lax.Precision.HIGHEST)
    term = lax.optimization_barrier(term.astype(jnp.bfloat16))
    moved = partner(term, dist).astype(jnp.float32)
    return jax.nn.relu(own_part + moved + bias[None]).astype(jnp.bfloat16)


def reference(source_field, self_weight, cross_weight, level_bias, switch_weight, switch_bias):
    distances = [STRIDE, NB // 2, NB // 4, 2 * STRIDE]
    field = source_field
    for layer_index in range(2):
        field = level_step(field, self_weight[layer_index], cross_weight[layer_index], level_bias[layer_index], distances[layer_index])
    shaped = field.reshape(SHOTS, NB // (GROUP * BLK_DEV), GROUP, BLK_DEV, GROUP, PIECE)
    mixed = jnp.transpose(shaped, (0, 1, 4, 3, 2, 5)).reshape(SHOTS, NB, W)
    product = jnp.einsum("sbi,bio->sbo", mixed.astype(jnp.float32), switch_weight.astype(jnp.float32), precision=lax.Precision.HIGHEST)
    field = jax.nn.relu(product + switch_bias[None]).astype(jnp.bfloat16)
    for layer_index in range(2, 4):
        field = level_step(field, self_weight[layer_index], cross_weight[layer_index], level_bias[layer_index], distances[layer_index])
    return field
```

```python
import jax
import jax.numpy as jnp
from jax import lax
from jax.experimental import pallas as pl
from jax.experimental.pallas import tpu as pltpu
from jax.sharding import PartitionSpec as P

UNITS = (1, 1, 2, 2, 2, 2, 2, 2, 1, 1)
F32, BF16 = jnp.float32, jnp.bfloat16
VMEM_BYTES = 16 << 20


def dot(a, b):
    return jnp.dot(a, b, preferred_element_type=F32)


def near(array):
    return dict(array=array, spec=pl.BlockSpec(memory_space=pltpu.VMEM))


def far(array):
    return dict(array=array, spec=pl.BlockSpec(memory_space=pltpu.HBM))


def scalar(array):
    return dict(array=array, spec=pl.BlockSpec(memory_space=pltpu.SMEM))


class Chain:
    def __init__(self):
        self.last = None

    def __call__(self, *stages):
        if not stages:
            return []
        anywhere = pl.BlockSpec(memory_space=pltpu.HBM)
        near = pl.BlockSpec(memory_space=pltpu.VMEM)
        operands, in_specs, out_shapes, out_specs, scratch, aliases = [], [], [], [], [], {}
        for stage in stages:
            for item in stage["ins"]:
                operands.append(item["array"])
                in_specs.append(item["spec"])
            if stage.get("into") is not None:
                aliases[len(operands)] = len(out_shapes)
                operands.append(stage["into"])
                in_specs.append(anywhere)
            for shape in stage["outs"]:
                out_shapes.append(jax.ShapeDtypeStruct(shape, BF16))
                out_specs.append(anywhere if "into" in stage else near)
            scratch += stage.get("scratch", [])
        if self.last is not None:
            operands.append(self.last)
            in_specs.append(pl.BlockSpec(memory_space=pl.ANY))
        n_in, n_out = len(operands), len(out_shapes)

        def kernel(*refs):
            ins, outs, tmp = list(refs[:n_in]), list(refs[n_in : n_in + n_out]), list(refs[n_in + n_out :])

            def take(refs, n):
                taken, refs[:n] = refs[:n], []
                return taken

            for stage in stages:
                given = take(ins, len(stage["ins"]))
                if stage.get("into") is not None:
                    take(ins, 1)
                stage["body"](given, take(outs, len(stage["outs"])), take(tmp, len(stage.get("scratch", []))))

        results = pl.pallas_call(
            kernel,
            out_shape=out_shapes,
            in_specs=in_specs,
            out_specs=out_specs,
            scratch_shapes=scratch,
            input_output_aliases=aliases,
            compiler_params=pltpu.CompilerParams(vmem_limit_bytes=VMEM_BYTES),
            cost_estimate=pl.CostEstimate(flops=1000, bytes_accessed=1000, transcendentals=0),
        )(*operands)
        self.last = results[0]
        grouped = []
        for stage in stages:
            grouped.append(results[: len(stage["outs"])])
            results = results[len(stage["outs"]) :]
        return grouped


def relu_sum(own, term, bias):
    return jnp.maximum(own + term.astype(F32) + bias, 0.0).astype(BF16)


def swap(value, axis, bit):
    return lax.ppermute(value, axis, [(i, i ^ 1 << bit) for i in range(lax.axis_size(axis))])


def pipelined(source_field, self_weight, cross_weight, level_bias, switch_weight, switch_bias):
    high_bit = lax.axis_size("src").bit_length() - 2
    pair_bit = high_bit - 1
    shots, blocks, width = source_field.shape
    half, piece = blocks // 2, width // 4
    packed = 128 // piece
    unit = shots // sum(UNITS)
    sizes = [unit * n for n in UNITS]
    starts = [sum(sizes[:t]) for t in range(len(sizes))]
    column, row = lax.axis_index("tgt") & 1, lax.axis_index("tgt") >> 1
    side = (lax.axis_index("src") >> pair_bit) & 1
    place = jnp.stack([side, row, column]).astype(jnp.int32)
    chain = Chain()

    def half_of(array, which):
        return lax.dynamic_slice_in_dim(array[2:4], which * half, half, 1)

    mine = jnp.concatenate([half_of(self_weight, side), half_of(cross_weight, side)])
    theirs = swap(
        jnp.concatenate([half_of(self_weight, 1 - side), half_of(cross_weight, 1 - side)]), "src", pair_bit
    )
    my_bias = half_of(level_bias, side)
    their_bias = swap(half_of(level_bias, 1 - side), "src", pair_bit)

    def first(start, size):
        step = 128 if size % 128 == 0 else size

        def body(ins, outs, tmp):
            x, cross = ins
            rows, sent = outs
            part, flat, sems = tmp
            copies = [
                pltpu.make_async_copy(x.at[pl.ds(start + at, step)], part.at[pl.ds(at, step)], sems.at[at // step])
                for at in range(0, size, step)
            ]
            for copy in copies:
                copy.start()
            for at, copy in zip(range(0, size, step), copies, strict=True):
                copy.wait()
                for c in range(width // 128):
                    lanes = part[at : at + step, :, c * 128 : (c + 1) * 128]
                    flat[c] = lanes.astype(F32).reshape(step * blocks, 128)
                for b in range(blocks):
                    lanes = [flat[c, pl.ds(b, step, stride=blocks), :] for c in range(width // 128)]
                    field = jnp.concatenate(lanes, axis=1).astype(BF16)
                    rows[b, at : at + step] = field
                    sent[b, at : at + step] = dot(field, cross[0, b]).astype(BF16)

        return dict(
            ins=[far(source_field), near(cross_weight)],
            outs=[(blocks, size, width), (blocks, size, width)],
            scratch=[
                pltpu.VMEM((size, blocks, width), BF16),
                pltpu.VMEM((width // 128, step * blocks, 128), F32),
                pltpu.SemaphoreType.DMA((size // step,)),
            ],
            body=body,
        )

    def second(rows, term, start, size):
        def body(ins, outs, tmp):
            x, got, own_w, bias, cross = ins
            hidden, sent = outs
            rows = slice(start, start + size)
            for b in range(blocks):
                h = relu_sum(dot(x[b, rows], own_w[0, b]), got[b, rows], bias[0, b : b + 1, :])
                hidden[b] = h
                sent[b] = dot(h, cross[1, b]).astype(BF16)

        return dict(
            ins=[
                near(rows),
                near(term),
                near(self_weight),
                near(level_bias),
                near(cross_weight),
            ],
            outs=[(blocks, size, width), (blocks, size, width)],
            body=body,
        )

    def third(hidden, term, size):
        def body(ins, outs, tmp):
            x, got, own_w, bias, where = ins
            sent, kept = outs
            (pieces,) = tmp
            for b in range(0, blocks, packed):
                group = [
                    relu_sum(dot(x[c], own_w[1, c]), got[c], bias[1, c : c + 1, :]).astype(F32)
                    for c in range(b, b + packed)
                ]
                for j in range(4):
                    lanes = [h[:, j * piece : (j + 1) * piece] for h in group]
                    pieces[j, b // packed] = jnp.concatenate(lanes, axis=1).astype(BF16)
            for c in range(2):
                sent[c] = pieces[(1 - where[1]) * 2 + c]
                kept[c] = pieces[where[1] * 2 + c]

        shape = (2, blocks // packed, size, 128)
        return dict(
            ins=[near(hidden), near(term), near(self_weight), near(level_bias), scalar(place)],
            outs=[shape, shape],
            scratch=[pltpu.VMEM((4, *shape[1:]), BF16)],
            body=body,
        )

    def between(kept, came):
        def body(ins, outs, tmp):
            x, y, where = ins
            (sent,) = outs
            for i, pieces in enumerate((x, y)):
                sent[i] = pieces[1 - where[2]]

        return dict(
            ins=[near(kept), near(came), scalar(place)],
            outs=[kept.shape],
            body=body,
        )

    def fourth(kept, came, came_last, size):
        def body(ins, outs, tmp):
            x, y, z, weight, bias, where = ins
            own, sent = outs
            pieces, full = tmp
            row, column = where[1], where[2]
            pieces[row * 2 + column] = x[column]
            pieces[(1 - row) * 2 + column] = y[column]
            pieces[row * 2 + 1 - column] = z[0]
            pieces[(1 - row) * 2 + 1 - column] = z[1]
            for b in range(blocks):
                at = b % packed * piece
                lanes = [pieces[g, b // packed].astype(F32)[:, at : at + piece] for g in range(4)]
                mixed = jnp.concatenate(lanes, axis=1).astype(BF16)
                full[b] = jnp.maximum(dot(mixed, weight[b]) + bias[b : b + 1, :], 0.0).astype(BF16)
            here = where[0]
            for b in range(half):
                sent[b] = full[(1 - here) * half + b]
                own[b] = full[here * half + b]

        return dict(
            ins=[near(kept), near(came), near(came_last), near(switch_weight), near(switch_bias), scalar(place)],
            outs=[(half, size, width), (half, size, width)],
            scratch=[
                pltpu.VMEM((4, blocks // packed, size, 128), BF16),
                pltpu.VMEM((blocks, size, width), BF16),
            ],
            body=body,
        )

    def fifth(kept, came, size):
        def body(ins, outs, tmp):
            x, y = ins[:2]
            w, v, wb, vb = ins[2:]
            own, other = outs
            for b in range(half):
                a, c = x[b], y[b]
                for k in range(2):
                    bias_a, bias_c = wb[k, b : b + 1, :], vb[k, b : b + 1, :]
                    term_a, term_c = dot(a, w[2 + k, b]).astype(BF16), dot(c, v[2 + k, b]).astype(BF16)
                    a, c = (
                        relu_sum(dot(a, w[k, b]), term_c, bias_a),
                        relu_sum(dot(c, v[k, b]), term_a, bias_c),
                    )
                own[b] = a
                other[b] = c

        weights = [near(array) for array in (mine, theirs, my_bias, their_bias)]
        return dict(
            ins=[near(kept), near(came), *weights],
            outs=[(half, size, width), (half, size, width)],
            body=body,
        )

    def sixth(start, own, came, out, size):
        def body(ins, outs, tmp):
            x, y, where = ins
            (result,) = outs
            flat, laid, sem = tmp
            here = where[0]
            for b in range(half):
                mine, other = x[b].astype(F32), y[b].astype(F32)
                for c in range(width // 128):
                    lanes = slice(c * 128, (c + 1) * 128)
                    flat[c, pl.ds(here * half + b, size, stride=blocks), :] = mine[:, lanes]
                    flat[c, pl.ds((1 - here) * half + b, size, stride=blocks), :] = other[:, lanes]
            for c in range(width // 128):
                lanes = slice(c * 128, (c + 1) * 128)
                laid[:, :, lanes] = flat[c].reshape(size, blocks, 128).astype(BF16)
            copy = pltpu.make_async_copy(laid, result.at[pl.ds(start, size)], sem)
            copy.start()
            copy.wait()

        return dict(
            ins=[near(own), near(came), scalar(place)],
            into=out,
            outs=[(shots, blocks, width)],
            scratch=[
                pltpu.VMEM((width // 128, size * blocks, 128), F32),
                pltpu.VMEM((size, blocks, width), BF16),
                pltpu.SemaphoreType.DMA,
            ],
            body=body,
        )

    count = len(sizes)
    state = {}
    out = None

    def run(*names):
        nonlocal out
        names = [(name, t) for name, t in names if 0 <= t < count]
        stages = []
        for name, t in names:
            size = sizes[t]
            if name == "first":
                stages.append(first(0, sizes[0]) if t == 0 else first(sizes[0], shots - sizes[0]))
            elif name == "second":
                start = 0 if t == 0 else starts[t] - sizes[0]
                stages.append(second(*state["first", min(t, 1)], start, size))
            elif name == "third":
                stages.append(third(*state.pop(("second", t)), size))
            elif name == "between":
                stages.append(between(*state["third", t]))
            elif name == "fourth":
                stages.append(fourth(*state.pop(("third", t)), state.pop(("between", t)), size))
            elif name == "fifth":
                stages.append(fifth(*state.pop(("fourth", t)), size))
            else:
                stages.append(sixth(starts[t], *state.pop(("fifth", t)), out, size))
        for (name, t), got in zip(names, chain(*stages), strict=True):
            if name == "first":
                state[name, t] = got[0], swap(got[1], "src", 0)
            elif name == "second":
                state[name, t] = got[0], swap(got[1], "src", high_bit)
            elif name == "third":
                state[name, t] = got[1], swap(got[0], "tgt", 1)
            elif name == "between":
                state[name, t] = swap(got[0], "tgt", 0)
            elif name in ("fourth", "fifth"):
                state[name, t] = got[0], swap(got[1], "src", pair_bit)
            else:
                (out,) = got

    run(("first", 0))
    run(("second", 0))
    run(("first", 1))
    run(("second", 1))
    for t in range(count + 3):
        run(("third", t), ("second", t + 2), ("sixth", t - 3))
        run(("fifth", t - 2))
        run(("fourth", t - 1))
        run(("between", t))
    return out


def level_step(field, self_w, cross_w, bias, bit):
    own = jnp.einsum("sbi,bio->sbo", field, self_w, preferred_element_type=F32)
    term = jnp.einsum("sbi,bio->sbo", field, cross_w, preferred_element_type=F32).astype(BF16)
    return relu_sum(own, swap(term, "src", bit), bias[None])


def stepwise(source_field, self_weight, cross_weight, level_bias, switch_weight, switch_bias):
    high_bit = lax.axis_size("src").bit_length() - 2
    bits = [0, high_bit, high_bit - 1, 1]
    field = source_field
    for k in range(4):
        field = level_step(field, self_weight[k], cross_weight[k], level_bias[k], bits[k])
        if k == 1:
            mixed = lax.all_to_all(field, "tgt", split_axis=2, concat_axis=2, tiled=True)
            product = jnp.einsum("sbi,bio->sbo", mixed, switch_weight, preferred_element_type=F32)
            field = jnp.maximum(product + switch_bias[None], 0.0).astype(BF16)
    return field


def solution(mesh):
    placed = (
        P(None, ("src", "tgt"), None),
        P(None, ("src", "tgt"), None, None),
        P(None, ("src", "tgt"), None, None),
        P(None, ("src", "tgt"), None),
        P(("src", "tgt"), None, None),
        P(("src", "tgt"), None),
    )
    same_pairs = mesh.shape["src"].bit_length() - 3 == 1
    per_device = pipelined if same_pairs and mesh.shape["tgt"] == 4 else stepwise
    return jax.shard_map(
        per_device,
        mesh=mesh,
        in_specs=placed,
        out_specs=P(None, ("src", "tgt"), None),
        check_vma=False,
    )
```

```python
import jax
import jax.numpy as jnp
from jax import lax
from jax.experimental import pallas as pl
from jax.experimental.pallas import tpu as pltpu
from jax.sharding import PartitionSpec as P

UNITS = (2, 2, 2, 2, 2, 2, 2, 2)
EARLY = 3
F32, BF16 = jnp.float32, jnp.bfloat16
VMEM_BYTES = 5 << 20


def dot(a, b):
    return jnp.dot(a, b, preferred_element_type=F32)


def near(array):
    return dict(array=array, spec=pl.BlockSpec(memory_space=pltpu.VMEM))


def far(array):
    return dict(array=array, spec=pl.BlockSpec(memory_space=pltpu.HBM))


def scalar(array):
    return dict(array=array, spec=pl.BlockSpec(memory_space=pltpu.SMEM))


class Chain:
    def __init__(self):
        self.last = None

    def __call__(self, *stages, after=(), vmem=VMEM_BYTES):
        if not stages:
            return []
        anywhere = pl.BlockSpec(memory_space=pltpu.HBM)
        near = pl.BlockSpec(memory_space=pltpu.VMEM)
        operands, in_specs, out_shapes, out_specs, scratch, aliases = [], [], [], [], [], {}
        for stage in stages:
            for item in stage["ins"]:
                operands.append(item["array"])
                in_specs.append(item["spec"])
            if stage.get("into") is not None:
                aliases[len(operands)] = len(out_shapes)
                operands.append(stage["into"])
                in_specs.append(anywhere)
            for shape in stage["outs"]:
                out_shapes.append(jax.ShapeDtypeStruct(shape, BF16))
                out_specs.append(anywhere if "into" in stage else near)
            scratch += stage.get("scratch", [])
        for array in (*after, *([] if self.last is None else [self.last])):
            operands.append(array)
            in_specs.append(pl.BlockSpec(memory_space=pl.ANY))
        n_in, n_out = len(operands), len(out_shapes)

        def kernel(*refs):
            ins, outs, tmp = list(refs[:n_in]), list(refs[n_in : n_in + n_out]), list(refs[n_in + n_out :])

            def take(refs, n):
                taken, refs[:n] = refs[:n], []
                return taken

            for stage in stages:
                given = take(ins, len(stage["ins"]))
                if stage.get("into") is not None:
                    take(ins, 1)
                stage["body"](given, take(outs, len(stage["outs"])), take(tmp, len(stage.get("scratch", []))))

        results = pl.pallas_call(
            kernel,
            out_shape=out_shapes,
            in_specs=in_specs,
            out_specs=out_specs,
            scratch_shapes=scratch,
            input_output_aliases=aliases,
            compiler_params=pltpu.CompilerParams(vmem_limit_bytes=vmem),
            cost_estimate=pl.CostEstimate(flops=1000, bytes_accessed=1000, transcendentals=0),
        )(*operands)
        self.last = results[0]
        grouped = []
        for stage in stages:
            grouped.append(results[: len(stage["outs"])])
            results = results[len(stage["outs"]) :]
        return grouped


def relu_sum(own, term, bias):
    return jnp.maximum(own + term.astype(F32) + bias, 0.0).astype(BF16)


def swap(value, axis, bit):
    return lax.ppermute(value, axis, [(i, i ^ 1 << bit) for i in range(lax.axis_size(axis))])


def pipelined(source_field, self_weight, cross_weight, level_bias, switch_weight, switch_bias):
    high_bit = lax.axis_size("src").bit_length() - 2
    pair_bit = high_bit - 1
    shots, blocks, width = source_field.shape
    half, piece = blocks // 2, width // 4
    packed = 128 // piece
    unit = shots // sum(UNITS)
    sizes = [unit * n for n in UNITS]
    starts = [sum(sizes[:t]) for t in range(len(sizes))]
    column, row = lax.axis_index("tgt") & 1, lax.axis_index("tgt") >> 1
    side = (lax.axis_index("src") >> pair_bit) & 1
    place = jnp.stack([side, row, column]).astype(jnp.int32)
    chain = Chain()

    def pack(i):
        def body(ins, outs, tmp):
            weight, bias, where = ins
            (sent,) = outs
            other = (1 - where[0]) * half
            for b in range(half):
                sent[b * width : (b + 1) * width] = weight[2 + i % 2, other + b]
            if i == 0:
                rows = []
                for row in [bias[2 + k, pl.ds(other + b, 1), :] for k in range(2) for b in range(half)]:
                    for _ in range(3):
                        rounded = row.astype(BF16).astype(F32)
                        rows.append(rounded)
                        row = row - rounded
                rows += [jnp.zeros_like(rows[0])] * (-len(rows) % 16)
                sent[half * width :] = jnp.concatenate(rows).astype(BF16)

        extra = -(-6 * half // 16) * 16 if i == 0 else 0
        return dict(
            ins=[near((self_weight, cross_weight)[i // 2]), near(level_bias), scalar(place)],
            outs=[(half * width + extra, width)],
            body=body,
        )

    def first(start, size):
        step = 128 if size % 128 == 0 else size

        def body(ins, outs, tmp):
            x, cross = ins
            rows, sent = outs
            (flat,) = tmp
            for at in range(0, size, step):
                for c in range(width // 128):
                    lanes = x[start + at : start + at + step, :, c * 128 : (c + 1) * 128]
                    flat[c] = lanes.astype(F32).reshape(step * blocks, 128)
                for b in range(blocks):
                    lanes = [flat[c, pl.ds(b, step, stride=blocks), :] for c in range(width // 128)]
                    field = jnp.concatenate(lanes, axis=1).astype(BF16)
                    rows[b, at : at + step] = field
                    sent[b, at : at + step] = dot(field, cross[0, b]).astype(BF16)

        return dict(
            ins=[near(source_field), near(cross_weight)],
            outs=[(blocks, size, width), (blocks, size, width)],
            scratch=[pltpu.VMEM((width // 128, step * blocks, 128), F32)],
            body=body,
        )

    def second(rows, term, start, size):
        def body(ins, outs, tmp):
            x, got, own_w, bias, cross = ins
            hidden, sent = outs
            rows = slice(start, start + size)
            for b in range(blocks):
                h = relu_sum(dot(x[b, rows], own_w[0, b]), got[b, rows], bias[0, b : b + 1, :])
                hidden[b] = h
                sent[b] = dot(h, cross[1, b]).astype(BF16)

        return dict(
            ins=[
                near(rows),
                near(term),
                near(self_weight),
                near(level_bias),
                near(cross_weight),
            ],
            outs=[(blocks, size, width), (blocks, size, width)],
            body=body,
        )

    def third(hidden, term, size):
        def body(ins, outs, tmp):
            x, got, own_w, bias, where = ins
            sent, kept = outs
            (pieces,) = tmp
            for b in range(0, blocks, packed):
                group = [
                    relu_sum(dot(x[c], own_w[1, c]), got[c], bias[1, c : c + 1, :]).astype(F32)
                    for c in range(b, b + packed)
                ]
                for j in range(4):
                    lanes = [h[:, j * piece : (j + 1) * piece] for h in group]
                    pieces[j, b // packed] = jnp.concatenate(lanes, axis=1).astype(BF16)
            for c in range(2):
                sent[c] = pieces[(1 - where[1]) * 2 + c]
                kept[c] = pieces[where[1] * 2 + c]

        shape = (2, blocks // packed, size, 128)
        return dict(
            ins=[near(hidden), near(term), near(self_weight), near(level_bias), scalar(place)],
            outs=[shape, shape],
            scratch=[pltpu.VMEM((4, *shape[1:]), BF16)],
            body=body,
        )

    def between(kept, came):
        def body(ins, outs, tmp):
            x, y, where = ins
            (sent,) = outs
            for i, pieces in enumerate((x, y)):
                sent[i] = pieces[1 - where[2]]

        return dict(
            ins=[near(kept), near(came), scalar(place)],
            outs=[kept.shape],
            body=body,
        )

    def fourth(kept, came, came_last, size):
        def body(ins, outs, tmp, message, at):
            x, y, z, weight, bias, where = ins
            (own,) = outs
            pieces, full = tmp
            row, column = where[1], where[2]
            pieces[row * 2 + column] = x[column]
            pieces[(1 - row) * 2 + column] = y[column]
            pieces[row * 2 + 1 - column] = z[0]
            pieces[(1 - row) * 2 + 1 - column] = z[1]
            for b in range(blocks):
                lane = b % packed * piece
                lanes = [pieces[g, b // packed].astype(F32)[:, lane : lane + piece] for g in range(4)]
                mixed = jnp.concatenate(lanes, axis=1).astype(BF16)
                full[b] = jnp.maximum(dot(mixed, weight[b]) + bias[b : b + 1, :], 0.0).astype(BF16)
            here = where[0]
            for b in range(half):
                message[at + b * size : at + (b + 1) * size] = full[(1 - here) * half + b]
                own[b] = full[here * half + b]

        return dict(
            ins=[near(kept), near(came), near(came_last), near(switch_weight), near(switch_bias), scalar(place)],
            outs=[(half, size, width)],
            scratch=[
                pltpu.VMEM((4, blocks // packed, size, 128), BF16),
                pltpu.VMEM((blocks, size, width), BF16),
            ],
            body=body,
        )

    def fifth(kept, came, start, size):
        def body(ins, outs, tmp, message, at):
            x, y = ins[:2]
            bias, where, self_w, cross_w = ins[2:6]
            v = ins[6:]
            their_bias = v[0][half * width :].astype(F32)
            here = where[0] * half
            (own,) = outs
            for b in range(half):
                a, c = x[b], y[start + b * size : start + (b + 1) * size]
                for k in range(2):
                    bias_a = bias[2 + k, pl.ds(here + b, 1), :]
                    row = 3 * (k * half + b)
                    bias_c = their_bias[row : row + 1] + their_bias[row + 1 : row + 2] + their_bias[row + 2 : row + 3]
                    term_a = dot(a, cross_w[2 + k, here + b]).astype(BF16)
                    term_c = dot(c, v[2 + k][b * width : (b + 1) * width]).astype(BF16)
                    a, c = (
                        relu_sum(dot(a, self_w[2 + k, here + b]), term_c, bias_a),
                        relu_sum(dot(c, v[k][b * width : (b + 1) * width]), term_a, bias_c),
                    )
                own[b] = a
                message[at + b * size : at + (b + 1) * size] = c

        weights = [near(level_bias), scalar(place)]
        weights += [near(self_weight), near(cross_weight)]
        weights += [near(state["pack", i]) for i in range(4)]
        return dict(
            ins=[near(kept), near(came), *weights],
            outs=[(half, size, width)],
            body=body,
        )

    def exchange(stages):
        rows = [half * size for _, size in stages]
        parts = [stage for stage, _ in stages]

        def body(ins, outs, tmp):
            at = 0
            for n, stage in zip(rows, parts, strict=True):
                given = []
                for refs, kind in ((ins, "ins"), (outs, "outs"), (tmp, "scratch")):
                    many = len(stage.get(kind, []))
                    given.append(refs[:many])
                    del refs[:many]
                stage["body"](*given, message=outs[-1], at=at)
                at += n

        join = lambda kind: [item for stage in parts for item in stage.get(kind, [])]
        return dict(ins=join("ins"), outs=[*join("outs"), (sum(rows), width)], scratch=join("scratch"), body=body)

    def sixth(start, own, came, first_row, out, size):
        def body(ins, outs, tmp):
            x, y, where = ins
            (result,) = outs
            flat, laid, sem = tmp
            here = where[0]
            for b in range(half):
                mine = x[b].astype(F32)
                other = y[first_row + b * size : first_row + (b + 1) * size].astype(F32)
                for c in range(width // 128):
                    lanes = slice(c * 128, (c + 1) * 128)
                    flat[c, pl.ds(here * half + b, size, stride=blocks), :] = mine[:, lanes]
                    flat[c, pl.ds((1 - here) * half + b, size, stride=blocks), :] = other[:, lanes]
            for c in range(width // 128):
                lanes = slice(c * 128, (c + 1) * 128)
                laid[:, :, lanes] = flat[c].reshape(size, blocks, 128).astype(BF16)
            copy = pltpu.make_async_copy(laid, result.at[pl.ds(start, size)], sem)
            copy.start()
            copy.wait()

        return dict(
            ins=[near(own), near(came), scalar(place)],
            into=out,
            outs=[(shots, blocks, width)],
            scratch=[
                pltpu.VMEM((width // 128, size * blocks, 128), F32),
                pltpu.VMEM((size, blocks, width), BF16),
                pltpu.SemaphoreType.DMA,
            ],
            body=body,
        )

    count = len(sizes)
    early = sum(sizes[:EARLY])
    state = {}
    out = None

    def run(*names, after=(), vmem=VMEM_BYTES):
        nonlocal out
        inside = lambda t: 0 <= t < count
        names = [(name, tuple(one for one in t if inside(one[1]))) if name == "swap" else (name, t) for name, t in names]
        names = [(name, t) for name, t in names if (t if name == "swap" else name == "pack" or inside(t))]
        stages = []
        for name, t in names:
            size = None if name == "swap" else sizes[t]
            if name == "first":
                stages.append(first(0, early) if t == 0 else first(early, shots - early))
            elif name == "second":
                late = starts[t] >= early
                stages.append(second(*state["first", int(late)], starts[t] - late * early, size))
            elif name == "third":
                stages.append(third(*state.pop(("second", t)), size))
            elif name == "between":
                stages.append(between(*state["third", t]))
            elif name == "pack":
                stages.append(pack(t))
            elif name == "swap":
                pairs = []
                for kind, u in t:
                    if kind == "fourth":
                        stage = fourth(*state.pop(("third", u)), state.pop(("between", u)), sizes[u])
                    else:
                        stage = fifth(*state.pop(("fourth", u)), sizes[u])
                    pairs.append((stage, sizes[u]))
                stages.append(exchange(pairs))
            else:
                stages.append(sixth(starts[t], *state.pop(("fifth", t)), out, size))
        for (name, t), got in zip(names, chain(*stages, after=after, vmem=vmem), strict=True):
            if name == "first":
                state[name, t] = got[0], swap(got[1], "src", 0)
            elif name == "second":
                state[name, t] = got[0], swap(got[1], "src", high_bit)
            elif name == "third":
                state[name, t] = got[1], swap(got[0], "tgt", 1)
            elif name == "between":
                state[name, t] = swap(got[0], "tgt", 0)
            elif name == "pack":
                state[name, t] = swap(got[0], "src", pair_bit)
            elif name == "swap":
                came, at = swap(got[-1], "src", pair_bit), 0
                for (kind, u), own in zip(t, got[:-1], strict=True):
                    state[kind, u] = own, came, at
                    at += half * sizes[u]
            else:
                (out,) = got

    run(("pack", 0))
    run(("first", 0))
    run(("second", 0))
    run(("second", 1), ("second", 2))
    run(("pack", 2))
    run(("third", 0), after=(state["pack", 0],))
    run(("first", 1))
    run(("pack", 1))
    run(("between", 0))
    run(("third", 1), after=(state["pack", 2],))
    run(("pack", 3), ("second", 3))
    run(("between", 1))
    run(("third", 2), ("second", 4), after=(state["pack", 1],))
    run(("swap", (("fourth", 0), ("fourth", 1))))
    run(("between", 2))
    run(("third", 3), ("second", 5), after=(state["pack", 3],))
    for t in range(3, count + 3):
        if t > 3:
            run(("third", t), ("second", t + 2))
        run(("swap", (("fourth", t - 1), ("fifth", t - 3))))
        run(("between", t), ("sixth", t - 5))
    for t in range(count - 2, count):
        run(("sixth", t))
    return out


def level_step(field, self_w, cross_w, bias, bit):
    own = jnp.einsum("sbi,bio->sbo", field, self_w, preferred_element_type=F32)
    term = jnp.einsum("sbi,bio->sbo", field, cross_w, preferred_element_type=F32).astype(BF16)
    return relu_sum(own, swap(term, "src", bit), bias[None])


def stepwise(source_field, self_weight, cross_weight, level_bias, switch_weight, switch_bias):
    high_bit = lax.axis_size("src").bit_length() - 2
    bits = [0, high_bit, high_bit - 1, 1]
    field = source_field
    for k in range(4):
        field = level_step(field, self_weight[k], cross_weight[k], level_bias[k], bits[k])
        if k == 1:
            mixed = lax.all_to_all(field, "tgt", split_axis=2, concat_axis=2, tiled=True)
            product = jnp.einsum("sbi,bio->sbo", mixed, switch_weight, preferred_element_type=F32)
            field = jnp.maximum(product + switch_bias[None], 0.0).astype(BF16)
    return field


def solution(mesh):
    placed = (
        P(None, ("src", "tgt"), None),
        P(None, ("src", "tgt"), None, None),
        P(None, ("src", "tgt"), None, None),
        P(None, ("src", "tgt"), None),
        P(("src", "tgt"), None, None),
        P(("src", "tgt"), None),
    )
    same_pairs = mesh.shape["src"].bit_length() - 3 == 1
    per_device = pipelined if same_pairs and mesh.shape["tgt"] == 4 else stepwise
    return jax.shard_map(
        per_device,
        mesh=mesh,
        in_specs=placed,
        out_specs=P(None, ("src", "tgt"), None),
        check_vma=False,
    )
```

```python
import jax
import jax.numpy as jnp
from jax import lax
from jax.experimental import pallas as pl
from jax.experimental.pallas import tpu as pltpu
from jax.sharding import PartitionSpec as P

UNITS = (2,2,2,2,2,2,2,2)
EARLY = 8
F32, BF16 = jnp.float32, jnp.bfloat16
VMEM_BYTES = 5 << 20


def dot(a, b):
    return jnp.dot(a, b, preferred_element_type=F32)


def near(array):
    return dict(array=array, spec=pl.BlockSpec(memory_space=pltpu.VMEM))


def far(array):
    return dict(array=array, spec=pl.BlockSpec(memory_space=pltpu.HBM))


def scalar(array):
    return dict(array=array, spec=pl.BlockSpec(memory_space=pltpu.SMEM))


class Chain:
    def __init__(self):
        self.last = None

    def __call__(self, *stages, after=(), vmem=VMEM_BYTES):
        if not stages:
            return []
        anywhere = pl.BlockSpec(memory_space=pltpu.HBM)
        near = pl.BlockSpec(memory_space=pltpu.VMEM)
        operands, in_specs, out_shapes, out_specs, scratch, aliases = [], [], [], [], [], {}
        for stage in stages:
            for item in stage["ins"]:
                operands.append(item["array"])
                in_specs.append(item["spec"])
            if stage.get("into") is not None:
                aliases[len(operands)] = len(out_shapes)
                operands.append(stage["into"])
                in_specs.append(anywhere)
            for shape in stage["outs"]:
                out_shapes.append(jax.ShapeDtypeStruct(shape, BF16))
                out_specs.append(anywhere if "into" in stage else near)
            scratch += stage.get("scratch", [])
        for array in (*after, *([] if self.last is None else [self.last])):
            operands.append(array)
            in_specs.append(pl.BlockSpec(memory_space=pl.ANY))
        n_in, n_out = len(operands), len(out_shapes)

        def kernel(*refs):
            ins, outs, tmp = list(refs[:n_in]), list(refs[n_in : n_in + n_out]), list(refs[n_in + n_out :])

            def take(refs, n):
                taken, refs[:n] = refs[:n], []
                return taken

            for stage in stages:
                given = take(ins, len(stage["ins"]))
                if stage.get("into") is not None:
                    take(ins, 1)
                stage["body"](given, take(outs, len(stage["outs"])), take(tmp, len(stage.get("scratch", []))))

        results = pl.pallas_call(
            kernel,
            out_shape=out_shapes,
            in_specs=in_specs,
            out_specs=out_specs,
            scratch_shapes=scratch,
            input_output_aliases=aliases,
            compiler_params=pltpu.CompilerParams(vmem_limit_bytes=vmem),
            cost_estimate=pl.CostEstimate(flops=1000, bytes_accessed=1000, transcendentals=0),
        )(*operands)
        self.last = results[0]
        grouped = []
        for stage in stages:
            grouped.append(results[: len(stage["outs"])])
            results = results[len(stage["outs"]) :]
        return grouped


def relu_sum(own, term, bias):
    return jnp.maximum(own + term.astype(F32) + bias, 0.0).astype(BF16)


def swap(value, axis, bit):
    return lax.ppermute(value, axis, [(i, i ^ 1 << bit) for i in range(lax.axis_size(axis))])


def pipelined(source_field, self_weight, cross_weight, level_bias, switch_weight, switch_bias):
    high_bit = lax.axis_size("src").bit_length() - 2
    pair_bit = high_bit - 1
    shots, blocks, width = source_field.shape
    half, piece = blocks // 2, width // 4
    packed = 128 // piece
    unit = shots // sum(UNITS)
    sizes = [unit * n for n in UNITS]
    starts = [sum(sizes[:t]) for t in range(len(sizes))]
    column, row = lax.axis_index("tgt") & 1, lax.axis_index("tgt") >> 1
    side = (lax.axis_index("src") >> pair_bit) & 1
    place = jnp.stack([side, row, column]).astype(jnp.int32)
    chain = Chain()

    cuts = (0, 2, 4)

    def pack(i):
        def body(ins, outs, tmp):
            self_w, cross_w, bias, where = ins
            (sent,) = outs
            other = (1 - where[0]) * half
            at = 0
            for weight, k in ((self_w, 2), (cross_w, 2), (self_w, 3), (cross_w, 3))[cuts[i] : cuts[i + 1]]:
                for b in range(half):
                    sent[at : at + width] = weight[k, other + b]
                    at += width
            if i > 0:
                return
            rows = []
            for row in [bias[2 + k, pl.ds(other + b, 1), :] for k in range(2) for b in range(half)]:
                for _ in range(3):
                    rounded = row.astype(BF16).astype(F32)
                    rows.append(rounded)
                    row = row - rounded
            rows += [jnp.zeros_like(rows[0])] * (-len(rows) % 16)
            sent[at:] = jnp.concatenate(rows).astype(BF16)

        extra = -(-6 * half // 16) * 16 if i == 0 else 0
        return dict(
            ins=[near(self_weight), near(cross_weight), near(level_bias), scalar(place)],
            outs=[((cuts[i + 1] - cuts[i]) * half * width + extra, width)],
            body=body,
        )

    def first(start, size):
        step = 128 if size % 128 == 0 else size

        def body(ins, outs, tmp):
            x, cross = ins
            rows, sent = outs
            (flat,) = tmp
            for at in range(0, size, step):
                for c in range(width // 128):
                    lanes = x[start + at : start + at + step, :, c * 128 : (c + 1) * 128]
                    flat[c] = lanes.astype(F32).reshape(step * blocks, 128)
                for b in range(blocks):
                    lanes = [flat[c, pl.ds(b, step, stride=blocks), :] for c in range(width // 128)]
                    field = jnp.concatenate(lanes, axis=1).astype(BF16)
                    rows[b, at : at + step] = field
                    sent[b, at : at + step] = dot(field, cross[0, b]).astype(BF16)

        return dict(
            ins=[near(source_field), near(cross_weight)],
            outs=[(blocks, size, width), (blocks, size, width)],
            scratch=[pltpu.VMEM((width // 128, step * blocks, 128), F32)],
            body=body,
        )

    def second(rows, term, start, size):
        def body(ins, outs, tmp):
            x, got, own_w, bias, cross = ins
            hidden, sent = outs
            rows = slice(start, start + size)
            for b in range(blocks):
                h = relu_sum(dot(x[b, rows], own_w[0, b]), got[b, rows], bias[0, b : b + 1, :])
                hidden[b] = h
                sent[b] = dot(h, cross[1, b]).astype(BF16)

        return dict(
            ins=[
                near(rows),
                near(term),
                near(self_weight),
                near(level_bias),
                near(cross_weight),
            ],
            outs=[(blocks, size, width), (blocks, size, width)],
            body=body,
        )

    def third(hidden, term, size):
        def body(ins, outs, tmp):
            x, got, own_w, bias, where = ins
            sent, kept = outs
            (pieces,) = tmp
            for b in range(0, blocks, packed):
                group = [
                    relu_sum(dot(x[c], own_w[1, c]), got[c], bias[1, c : c + 1, :]).astype(F32)
                    for c in range(b, b + packed)
                ]
                for j in range(4):
                    lanes = [h[:, j * piece : (j + 1) * piece] for h in group]
                    pieces[j, b // packed] = jnp.concatenate(lanes, axis=1).astype(BF16)
            for c in range(2):
                sent[c] = pieces[(1 - where[1]) * 2 + c]
                kept[c] = pieces[where[1] * 2 + c]

        shape = (2, blocks // packed, size, 128)
        return dict(
            ins=[near(hidden), near(term), near(self_weight), near(level_bias), scalar(place)],
            outs=[shape, shape],
            scratch=[pltpu.VMEM((4, *shape[1:]), BF16)],
            body=body,
        )

    def between(kept, came):
        def body(ins, outs, tmp):
            x, y, where = ins
            (sent,) = outs
            for i, pieces in enumerate((x, y)):
                sent[i] = pieces[1 - where[2]]

        return dict(
            ins=[near(kept), near(came), scalar(place)],
            outs=[kept.shape],
            body=body,
        )

    def fourth(kept, came, came_last, size):
        def body(ins, outs, tmp, message, at):
            x, y, z, weight, bias, where = ins
            (own,) = outs
            pieces, full = tmp
            row, column = where[1], where[2]
            pieces[row * 2 + column] = x[column]
            pieces[(1 - row) * 2 + column] = y[column]
            pieces[row * 2 + 1 - column] = z[0]
            pieces[(1 - row) * 2 + 1 - column] = z[1]
            for b in range(blocks):
                lane = b % packed * piece
                lanes = [pieces[g, b // packed].astype(F32)[:, lane : lane + piece] for g in range(4)]
                mixed = jnp.concatenate(lanes, axis=1).astype(BF16)
                full[b] = jnp.maximum(dot(mixed, weight[b]) + bias[b : b + 1, :], 0.0).astype(BF16)
            here = where[0]
            for b in range(half):
                message[at + b * size : at + (b + 1) * size] = full[(1 - here) * half + b]
                own[b] = full[here * half + b]

        return dict(
            ins=[near(kept), near(came), near(came_last), near(switch_weight), near(switch_bias), scalar(place)],
            outs=[(half, size, width)],
            scratch=[
                pltpu.VMEM((4, blocks // packed, size, 128), BF16),
                pltpu.VMEM((blocks, size, width), BF16),
            ],
            body=body,
        )

    def fifth(kept, came, start, size):
        def body(ins, outs, tmp, message, at):
            x, y = ins[:2]
            bias, where, self_w, cross_w = ins[2:6]
            v = ins[6:]

            def theirs(i, b):
                n = int(i >= cuts[1])
                at = ((i - cuts[n]) * half + b) * width
                return v[n][at : at + width]

            their_bias = v[0][cuts[1] * half * width :].astype(F32)
            here = where[0] * half
            (own,) = outs
            for b in range(half):
                a, c = x[b], y[start + b * size : start + (b + 1) * size]
                for k in range(2):
                    bias_a = bias[2 + k, pl.ds(here + b, 1), :]
                    row = 3 * (k * half + b)
                    bias_c = their_bias[row : row + 1] + their_bias[row + 1 : row + 2] + their_bias[row + 2 : row + 3]
                    term_a = dot(a, cross_w[2 + k, here + b]).astype(BF16)
                    term_c = dot(c, theirs(2 * k + 1, b)).astype(BF16)
                    a, c = (
                        relu_sum(dot(a, self_w[2 + k, here + b]), term_c, bias_a),
                        relu_sum(dot(c, theirs(2 * k, b)), term_a, bias_c),
                    )
                own[b] = a
                message[at + b * size : at + (b + 1) * size] = c

        weights = [near(level_bias), scalar(place)]
        weights += [near(self_weight), near(cross_weight)]
        weights += [near(state["pack", i]) for i in range(2)]
        return dict(
            ins=[near(kept), near(came), *weights],
            outs=[(half, size, width)],
            body=body,
        )

    def exchange(stages):
        rows = [half * size for _, size in stages]
        parts = [stage for stage, _ in stages]

        def body(ins, outs, tmp):
            at = 0
            for n, stage in zip(rows, parts, strict=True):
                given = []
                for refs, kind in ((ins, "ins"), (outs, "outs"), (tmp, "scratch")):
                    many = len(stage.get(kind, []))
                    given.append(refs[:many])
                    del refs[:many]
                stage["body"](*given, message=outs[-1], at=at)
                at += n

        join = lambda kind: [item for stage in parts for item in stage.get(kind, [])]
        return dict(ins=join("ins"), outs=[*join("outs"), (sum(rows), width)], scratch=join("scratch"), body=body)

    def sixth(start, own, came, first_row, out, size):
        def body(ins, outs, tmp):
            x, y, where = ins
            (result,) = outs
            flat, laid, sem = tmp
            here = where[0]
            for b in range(half):
                mine = x[b].astype(F32)
                other = y[first_row + b * size : first_row + (b + 1) * size].astype(F32)
                for c in range(width // 128):
                    lanes = slice(c * 128, (c + 1) * 128)
                    flat[c, pl.ds(here * half + b, size, stride=blocks), :] = mine[:, lanes]
                    flat[c, pl.ds((1 - here) * half + b, size, stride=blocks), :] = other[:, lanes]
            for c in range(width // 128):
                lanes = slice(c * 128, (c + 1) * 128)
                laid[:, :, lanes] = flat[c].reshape(size, blocks, 128).astype(BF16)
            copy = pltpu.make_async_copy(laid, result.at[pl.ds(start, size)], sem)
            copy.start()
            copy.wait()

        return dict(
            ins=[near(own), near(came), scalar(place)],
            into=out,
            outs=[(shots, blocks, width)],
            scratch=[
                pltpu.VMEM((width // 128, size * blocks, 128), F32),
                pltpu.VMEM((size, blocks, width), BF16),
                pltpu.SemaphoreType.DMA,
            ],
            body=body,
        )

    count = len(sizes)
    early = sum(sizes[:EARLY])
    state = {}
    out = None

    def run(*names, after=(), vmem=VMEM_BYTES):
        nonlocal out
        inside = lambda t: 0 <= t < count
        names = [(name, tuple(one for one in t if inside(one[1]))) if name == "swap" else (name, t) for name, t in names]
        names = [(name, t) for name, t in names if (t if name == "swap" else name == "pack" or inside(t))]
        stages = []
        for name, t in names:
            size = None if name == "swap" else sizes[t]
            if name == "first":
                stages.append(first(0, early) if t == 0 else first(early, shots - early))
            elif name == "second":
                late = starts[t] >= early
                stages.append(second(*state["first", int(late)], starts[t] - late * early, size))
            elif name == "third":
                stages.append(third(*state.pop(("second", t)), size))
            elif name == "between":
                stages.append(between(*state["third", t]))
            elif name == "pack":
                stages.append(pack(t))
            elif name == "swap":
                pairs = []
                for kind, u in t:
                    if kind == "fourth":
                        stage = fourth(*state.pop(("third", u)), state.pop(("between", u)), sizes[u])
                    else:
                        stage = fifth(*state.pop(("fourth", u)), sizes[u])
                    pairs.append((stage, sizes[u]))
                stages.append(exchange(pairs))
            else:
                stages.append(sixth(starts[t], *state.pop(("fifth", t)), out, size))
        for (name, t), got in zip(names, chain(*stages, after=after, vmem=vmem), strict=True):
            if name == "first":
                state[name, t] = got[0], swap(got[1], "src", 0)
            elif name == "second":
                state[name, t] = got[0], swap(got[1], "src", high_bit)
            elif name == "third":
                state[name, t] = got[1], swap(got[0], "tgt", 1)
            elif name == "between":
                state[name, t] = swap(got[0], "tgt", 0)
            elif name == "pack":
                state[name, t] = swap(got[0], "src", pair_bit)
            elif name == "swap":
                came, at = swap(got[-1], "src", pair_bit), 0
                state["came"] = came
                for (kind, u), own in zip(t, got[:-1], strict=True):
                    state[kind, u] = own, came, at
                    at += half * sizes[u]
            else:
                (out,) = got

    run(("pack", 0))
    run(("first", 0))
    run(("second", 0))
    run(("second", 1))
    run(("second", 2))
    run(("second", 3))
    run(("pack", 1))
    run(("third", 0))
    run(("third", 1))
    run(("third", 2), after=(state["pack", 0],))
    run(("between", 0))
    run(("between", 1))
    run(("swap", (("fourth", 0), ("fourth", 1))))
    run(("between", 2), ("second", 4))
    run(("third", 3), ("second", 5), after=(state["pack", 1],))
    for t in range(3, count):
        if t > 3:
            run(("third", t), ("second", t + 2))
        last = state["came"]
        run(("swap", (("fourth", t - 1), ("fifth", t - 3))))
        run(("between", t), ("sixth", t - 5), after=(last,))
    run(("swap", (("fourth", count - 1),)))
    run(("sixth", count - 5))
    run(("swap", (("fifth", count - 3),)))
    run(("swap", (("fifth", count - 2),)))
    run(("sixth", count - 4))
    run(("swap", (("fifth", count - 1),)))
    run(("sixth", count - 3))
    run(("sixth", count - 2))
    run(("sixth", count - 1))
    return out


def level_step(field, self_w, cross_w, bias, bit):
    own = jnp.einsum("sbi,bio->sbo", field, self_w, preferred_element_type=F32)
    term = jnp.einsum("sbi,bio->sbo", field, cross_w, preferred_element_type=F32).astype(BF16)
    return relu_sum(own, swap(term, "src", bit), bias[None])


def stepwise(source_field, self_weight, cross_weight, level_bias, switch_weight, switch_bias):
    high_bit = lax.axis_size("src").bit_length() - 2
    bits = [0, high_bit, high_bit - 1, 1]
    field = source_field
    for k in range(4):
        field = level_step(field, self_weight[k], cross_weight[k], level_bias[k], bits[k])
        if k == 1:
            mixed = lax.all_to_all(field, "tgt", split_axis=2, concat_axis=2, tiled=True)
            product = jnp.einsum("sbi,bio->sbo", mixed, switch_weight, preferred_element_type=F32)
            field = jnp.maximum(product + switch_bias[None], 0.0).astype(BF16)
    return field


def solution(mesh):
    placed = (
        P(None, ("src", "tgt"), None),
        P(None, ("src", "tgt"), None, None),
        P(None, ("src", "tgt"), None, None),
        P(None, ("src", "tgt"), None),
        P(("src", "tgt"), None, None),
        P(("src", "tgt"), None),
    )
    same_pairs = mesh.shape["src"].bit_length() - 3 == 1
    per_device = pipelined if same_pairs and mesh.shape["tgt"] == 4 else stepwise
    return jax.shard_map(
        per_device,
        mesh=mesh,
        in_specs=placed,
        out_specs=P(None, ("src", "tgt"), None),
        check_vma=False,
    )
```

```python
import jax
import jax.numpy as jnp
from jax import lax
from jax.experimental import pallas as pl
from jax.experimental.pallas import tpu as pltpu
from jax.sharding import PartitionSpec as P

UNITS = (2,2,2,2,2,2,2,2)
EARLY = 8
F32, BF16 = jnp.float32, jnp.bfloat16
VMEM_BYTES = 5 << 20


def dot(a, b):
    return jnp.dot(a, b, preferred_element_type=F32)


def near(array):
    return dict(array=array, spec=pl.BlockSpec(memory_space=pltpu.VMEM))


def far(array):
    return dict(array=array, spec=pl.BlockSpec(memory_space=pltpu.HBM))


def scalar(array):
    return dict(array=array, spec=pl.BlockSpec(memory_space=pltpu.SMEM))


class Chain:
    def __init__(self):
        self.last = None

    def __call__(self, *stages, after=(), vmem=VMEM_BYTES):
        if not stages:
            return []
        anywhere = pl.BlockSpec(memory_space=pltpu.HBM)
        near = pl.BlockSpec(memory_space=pltpu.VMEM)
        operands, in_specs, out_shapes, out_specs, scratch, aliases = [], [], [], [], [], {}
        for stage in stages:
            for item in stage["ins"]:
                operands.append(item["array"])
                in_specs.append(item["spec"])
            if stage.get("into") is not None:
                aliases[len(operands)] = len(out_shapes)
                operands.append(stage["into"])
                in_specs.append(anywhere)
            for shape in stage["outs"]:
                out_shapes.append(jax.ShapeDtypeStruct(shape, BF16))
                out_specs.append(anywhere if "into" in stage else near)
            scratch += stage.get("scratch", [])
        for array in (*after, *([] if self.last is None else [self.last])):
            operands.append(array)
            in_specs.append(pl.BlockSpec(memory_space=pl.ANY))
        n_in, n_out = len(operands), len(out_shapes)

        def kernel(*refs):
            ins, outs, tmp = list(refs[:n_in]), list(refs[n_in : n_in + n_out]), list(refs[n_in + n_out :])

            def take(refs, n):
                taken, refs[:n] = refs[:n], []
                return taken

            for stage in stages:
                given = take(ins, len(stage["ins"]))
                if stage.get("into") is not None:
                    take(ins, 1)
                stage["body"](given, take(outs, len(stage["outs"])), take(tmp, len(stage.get("scratch", []))))

        results = pl.pallas_call(
            kernel,
            out_shape=out_shapes,
            in_specs=in_specs,
            out_specs=out_specs,
            scratch_shapes=scratch,
            input_output_aliases=aliases,
            compiler_params=pltpu.CompilerParams(vmem_limit_bytes=vmem),
            cost_estimate=pl.CostEstimate(flops=1000, bytes_accessed=1000, transcendentals=0),
        )(*operands)
        self.last = results[0]
        grouped = []
        for stage in stages:
            grouped.append(results[: len(stage["outs"])])
            results = results[len(stage["outs"]) :]
        return grouped


def relu_sum(own, term, bias):
    return jnp.maximum(own + term.astype(F32) + bias, 0.0).astype(BF16)


def swap(value, axis, bit):
    return lax.ppermute(value, axis, [(i, i ^ 1 << bit) for i in range(lax.axis_size(axis))])


def pipelined(source_field, self_weight, cross_weight, level_bias, switch_weight, switch_bias):
    high_bit = lax.axis_size("src").bit_length() - 2
    pair_bit = high_bit - 1
    shots, blocks, width = source_field.shape
    half, piece = blocks // 2, width // 4
    packed = 128 // piece
    unit = shots // sum(UNITS)
    sizes = [unit * n for n in UNITS]
    starts = [sum(sizes[:t]) for t in range(len(sizes))]
    column, row = lax.axis_index("tgt") & 1, lax.axis_index("tgt") >> 1
    side = (lax.axis_index("src") >> pair_bit) & 1
    place = jnp.stack([side, row, column]).astype(jnp.int32)
    chain = Chain()

    cuts = (0, 2, 4)

    def pack(i):
        def body(ins, outs, tmp):
            self_w, cross_w, bias, where = ins
            (sent,) = outs
            other = (1 - where[0]) * half
            at = 0
            for weight, k in ((self_w, 2), (cross_w, 2), (self_w, 3), (cross_w, 3))[cuts[i] : cuts[i + 1]]:
                for b in range(half):
                    sent[at : at + width] = weight[k, other + b]
                    at += width
            if i > 0:
                return
            rows = []
            for row in [bias[2 + k, pl.ds(other + b, 1), :] for k in range(2) for b in range(half)]:
                for _ in range(3):
                    rounded = row.astype(BF16).astype(F32)
                    rows.append(rounded)
                    row = row - rounded
            rows += [jnp.zeros_like(rows[0])] * (-len(rows) % 16)
            sent[at:] = jnp.concatenate(rows).astype(BF16)

        extra = -(-6 * half // 16) * 16 if i == 0 else 0
        return dict(
            ins=[near(self_weight), near(cross_weight), near(level_bias), scalar(place)],
            outs=[((cuts[i + 1] - cuts[i]) * half * width + extra, width)],
            body=body,
        )

    def first(start, size):
        step = 128 if size % 128 == 0 else size

        def body(ins, outs, tmp):
            x, cross = ins
            rows, sent = outs
            (flat,) = tmp
            for at in range(0, size, step):
                for c in range(width // 128):
                    lanes = x[start + at : start + at + step, :, c * 128 : (c + 1) * 128]
                    flat[c] = lanes.astype(F32).reshape(step * blocks, 128)
                for b in range(blocks):
                    lanes = [flat[c, pl.ds(b, step, stride=blocks), :] for c in range(width // 128)]
                    field = jnp.concatenate(lanes, axis=1).astype(BF16)
                    rows[b, at : at + step] = field
                    sent[b, at : at + step] = dot(field, cross[0, b]).astype(BF16)

        return dict(
            ins=[near(source_field), near(cross_weight)],
            outs=[(blocks, size, width), (blocks, size, width)],
            scratch=[pltpu.VMEM((width // 128, step * blocks, 128), F32)],
            body=body,
        )

    def second(rows, term, start, size):
        def body(ins, outs, tmp):
            x, got, own_w, bias, cross = ins
            hidden, sent = outs
            rows = slice(start, start + size)
            for b in range(blocks):
                h = relu_sum(dot(x[b, rows], own_w[0, b]), got[b, rows], bias[0, b : b + 1, :])
                hidden[b] = h
                sent[b] = dot(h, cross[1, b]).astype(BF16)

        return dict(
            ins=[
                near(rows),
                near(term),
                near(self_weight),
                near(level_bias),
                near(cross_weight),
            ],
            outs=[(blocks, size, width), (blocks, size, width)],
            body=body,
        )

    def third(hidden, term, size):
        def body(ins, outs, tmp):
            x, got, own_w, bias, where = ins
            sent, kept = outs
            (pieces,) = tmp
            for b in range(0, blocks, packed):
                group = [
                    relu_sum(dot(x[c], own_w[1, c]), got[c], bias[1, c : c + 1, :]).astype(F32)
                    for c in range(b, b + packed)
                ]
                for j in range(4):
                    lanes = [h[:, j * piece : (j + 1) * piece] for h in group]
                    pieces[j, b // packed] = jnp.concatenate(lanes, axis=1).astype(BF16)
            for c in range(2):
                sent[c] = pieces[(1 - where[1]) * 2 + c]
                kept[c] = pieces[where[1] * 2 + c]

        shape = (2, blocks // packed, size, 128)
        return dict(
            ins=[near(hidden), near(term), near(self_weight), near(level_bias), scalar(place)],
            outs=[shape, shape],
            scratch=[pltpu.VMEM((4, *shape[1:]), BF16)],
            body=body,
        )

    def between(kept, came):
        def body(ins, outs, tmp):
            x, y, where = ins
            (sent,) = outs
            for i, pieces in enumerate((x, y)):
                sent[i] = pieces[1 - where[2]]

        return dict(
            ins=[near(kept), near(came), scalar(place)],
            outs=[kept.shape],
            body=body,
        )

    def fourth(kept, came, came_last, size):
        def body(ins, outs, tmp, message, at):
            x, y, z, weight, bias, where = ins
            (own,) = outs
            pieces, full = tmp
            row, column = where[1], where[2]
            pieces[row * 2 + column] = x[column]
            pieces[(1 - row) * 2 + column] = y[column]
            pieces[row * 2 + 1 - column] = z[0]
            pieces[(1 - row) * 2 + 1 - column] = z[1]
            for b in range(blocks):
                lane = b % packed * piece
                lanes = [pieces[g, b // packed].astype(F32)[:, lane : lane + piece] for g in range(4)]
                mixed = jnp.concatenate(lanes, axis=1).astype(BF16)
                full[b] = jnp.maximum(dot(mixed, weight[b]) + bias[b : b + 1, :], 0.0).astype(BF16)
            here = where[0]
            for b in range(half):
                message[at + b * size : at + (b + 1) * size] = full[(1 - here) * half + b]
                own[b] = full[here * half + b]

        return dict(
            ins=[near(kept), near(came), near(came_last), near(switch_weight), near(switch_bias), scalar(place)],
            outs=[(half, size, width)],
            scratch=[
                pltpu.VMEM((4, blocks // packed, size, 128), BF16),
                pltpu.VMEM((blocks, size, width), BF16),
            ],
            body=body,
        )

    def fifth(kept, came, start, size):
        def body(ins, outs, tmp, message, at):
            x, y = ins[:2]
            bias, where, self_w, cross_w = ins[2:6]
            v = ins[6:]

            def theirs(i, b):
                n = int(i >= cuts[1])
                at = ((i - cuts[n]) * half + b) * width
                return v[n][at : at + width]

            their_bias = v[0][cuts[1] * half * width :].astype(F32)
            here = where[0] * half
            (own,) = outs
            for b in range(half):
                a, c = x[b], y[start + b * size : start + (b + 1) * size]
                for k in range(2):
                    bias_a = bias[2 + k, pl.ds(here + b, 1), :]
                    row = 3 * (k * half + b)
                    bias_c = their_bias[row : row + 1] + their_bias[row + 1 : row + 2] + their_bias[row + 2 : row + 3]
                    term_a = dot(a, cross_w[2 + k, here + b]).astype(BF16)
                    term_c = dot(c, theirs(2 * k + 1, b)).astype(BF16)
                    a, c = (
                        relu_sum(dot(a, self_w[2 + k, here + b]), term_c, bias_a),
                        relu_sum(dot(c, theirs(2 * k, b)), term_a, bias_c),
                    )
                own[b] = a
                message[at + b * size : at + (b + 1) * size] = c

        weights = [near(level_bias), scalar(place)]
        weights += [near(self_weight), near(cross_weight)]
        weights += [near(state["pack", i]) for i in range(2)]
        return dict(
            ins=[near(kept), near(came), *weights],
            outs=[(half, size, width)],
            body=body,
        )

    def exchange(stages):
        rows = [half * size for _, size in stages]
        parts = [stage for stage, _ in stages]

        def body(ins, outs, tmp):
            at = 0
            for n, stage in zip(rows, parts, strict=True):
                given = []
                for refs, kind in ((ins, "ins"), (outs, "outs"), (tmp, "scratch")):
                    many = len(stage.get(kind, []))
                    given.append(refs[:many])
                    del refs[:many]
                stage["body"](*given, message=outs[-1], at=at)
                at += n

        join = lambda kind: [item for stage in parts for item in stage.get(kind, [])]
        return dict(ins=join("ins"), outs=[*join("outs"), (sum(rows), width)], scratch=join("scratch"), body=body)

    def sixth(start, own, came, first_row, out, size):
        def body(ins, outs, tmp):
            x, y, where = ins
            (result,) = outs
            flat, laid, sem = tmp
            here = where[0]
            for b in range(half):
                mine = x[b].astype(F32)
                other = y[first_row + b * size : first_row + (b + 1) * size].astype(F32)
                for c in range(width // 128):
                    lanes = slice(c * 128, (c + 1) * 128)
                    flat[c, pl.ds(here * half + b, size, stride=blocks), :] = mine[:, lanes]
                    flat[c, pl.ds((1 - here) * half + b, size, stride=blocks), :] = other[:, lanes]
            for c in range(width // 128):
                lanes = slice(c * 128, (c + 1) * 128)
                laid[:, :, lanes] = flat[c].reshape(size, blocks, 128).astype(BF16)
            copy = pltpu.make_async_copy(laid, result.at[pl.ds(start, size)], sem)
            copy.start()
            copy.wait()

        return dict(
            ins=[near(own), near(came), scalar(place)],
            into=out,
            outs=[(shots, blocks, width)],
            scratch=[
                pltpu.VMEM((width // 128, size * blocks, 128), F32),
                pltpu.VMEM((size, blocks, width), BF16),
                pltpu.SemaphoreType.DMA,
            ],
            body=body,
        )

    count = len(sizes)
    early = sum(sizes[:EARLY])
    state = {}
    out = None

    def run(*names, after=(), vmem=VMEM_BYTES):
        nonlocal out
        inside = lambda t: 0 <= t < count
        names = [(name, tuple(one for one in t if inside(one[1]))) if name == "swap" else (name, t) for name, t in names]
        names = [(name, t) for name, t in names if (t if name == "swap" else name == "pack" or inside(t))]
        stages = []
        for name, t in names:
            size = None if name == "swap" else sizes[t]
            if name == "first":
                stages.append(first(0, early) if t == 0 else first(early, shots - early))
            elif name == "second":
                late = starts[t] >= early
                stages.append(second(*state["first", int(late)], starts[t] - late * early, size))
            elif name == "third":
                stages.append(third(*state.pop(("second", t)), size))
            elif name == "between":
                stages.append(between(*state["third", t]))
            elif name == "pack":
                stages.append(pack(t))
            elif name == "swap":
                pairs = []
                for kind, u in t:
                    if kind == "fourth":
                        stage = fourth(*state.pop(("third", u)), state.pop(("between", u)), sizes[u])
                    else:
                        stage = fifth(*state.pop(("fourth", u)), sizes[u])
                    pairs.append((stage, sizes[u]))
                stages.append(exchange(pairs))
            else:
                stages.append(sixth(starts[t], *state.pop(("fifth", t)), out, size))
        for (name, t), got in zip(names, chain(*stages, after=after, vmem=vmem), strict=True):
            if name == "first":
                state[name, t] = got[0], swap(got[1], "src", 0)
            elif name == "second":
                state[name, t] = got[0], swap(got[1], "src", high_bit)
            elif name == "third":
                state[name, t] = got[1], swap(got[0], "tgt", 1)
            elif name == "between":
                state[name, t] = swap(got[0], "tgt", 0)
            elif name == "pack":
                state[name, t] = swap(got[0], "src", pair_bit)
            elif name == "swap":
                came, at = swap(got[-1], "src", pair_bit), 0
                state["came"] = came
                for (kind, u), own in zip(t, got[:-1], strict=True):
                    state[kind, u] = own, came, at
                    at += half * sizes[u]
            else:
                (out,) = got

    run(("pack", 0))
    run(("first", 0))
    run(("second", 0))
    run(("second", 1))
    run(("second", 2))
    run(("pack", 1))
    run(("third", 0))
    run(("third", 1), after=(state["pack", 0],))
    run(("between", 0))
    run(("between", 1))
    run(("third", 2), ("second", 3), ("second", 4))
    run(("swap", (("fourth", 0), ("fourth", 1))))
    run(("between", 2), after=(state["pack", 1],))
    run(("third", 3), ("second", 5))
    for t in range(3, count):
        if t > 3:
            run(("third", t), ("second", t + 2))
        last = state["came"]
        run(("swap", (("fourth", t - 1), ("fifth", t - 3))))
        run(("between", t), ("sixth", t - 5), after=(last,))
    run(("swap", (("fourth", count - 1),)))
    run(("sixth", count - 5))
    run(("swap", (("fifth", count - 3),)))
    run(("swap", (("fifth", count - 2),)))
    run(("sixth", count - 4))
    run(("swap", (("fifth", count - 1),)))
    run(("sixth", count - 3))
    run(("sixth", count - 2))
    run(("sixth", count - 1))
    return out


def level_step(field, self_w, cross_w, bias, bit):
    own = jnp.einsum("sbi,bio->sbo", field, self_w, preferred_element_type=F32)
    term = jnp.einsum("sbi,bio->sbo", field, cross_w, preferred_element_type=F32).astype(BF16)
    return relu_sum(own, swap(term, "src", bit), bias[None])


def stepwise(source_field, self_weight, cross_weight, level_bias, switch_weight, switch_bias):
    high_bit = lax.axis_size("src").bit_length() - 2
    bits = [0, high_bit, high_bit - 1, 1]
    field = source_field
    for k in range(4):
        field = level_step(field, self_weight[k], cross_weight[k], level_bias[k], bits[k])
        if k == 1:
            mixed = lax.all_to_all(field, "tgt", split_axis=2, concat_axis=2, tiled=True)
            product = jnp.einsum("sbi,bio->sbo", mixed, switch_weight, preferred_element_type=F32)
            field = jnp.maximum(product + switch_bias[None], 0.0).astype(BF16)
    return field


def solution(mesh):
    placed = (
        P(None, ("src", "tgt"), None),
        P(None, ("src", "tgt"), None, None),
        P(None, ("src", "tgt"), None, None),
        P(None, ("src", "tgt"), None),
        P(("src", "tgt"), None, None),
        P(("src", "tgt"), None),
    )
    same_pairs = mesh.shape["src"].bit_length() - 3 == 1
    per_device = pipelined if same_pairs and mesh.shape["tgt"] == 4 else stepwise
    return jax.shard_map(
        per_device,
        mesh=mesh,
        in_specs=placed,
        out_specs=P(None, ("src", "tgt"), None),
        check_vma=False,
    )
```

```python
import jax
import jax.numpy as jnp
from jax import lax
from jax.experimental import pallas as pl
from jax.experimental.pallas import tpu as pltpu
from jax.sharding import PartitionSpec as P

UNITS = (2, 2, 2, 2, 2, 2, 2, 2)
EARLY = 8
F32, BF16 = jnp.float32, jnp.bfloat16
VMEM_BYTES = 5 << 20


def dot(a, b):
    return jnp.dot(a, b, preferred_element_type=F32)


def near(array):
    return dict(array=array, spec=pl.BlockSpec(memory_space=pltpu.VMEM))


def far(array):
    return dict(array=array, spec=pl.BlockSpec(memory_space=pltpu.HBM))


def scalar(array):
    return dict(array=array, spec=pl.BlockSpec(memory_space=pltpu.SMEM))


class Chain:
    def __init__(self):
        self.last = None

    def __call__(self, *stages, after=(), vmem=VMEM_BYTES):
        if not stages:
            return []
        anywhere = pl.BlockSpec(memory_space=pltpu.HBM)
        near = pl.BlockSpec(memory_space=pltpu.VMEM)
        operands, in_specs, out_shapes, out_specs, scratch, aliases = [], [], [], [], [], {}
        for stage in stages:
            for item in stage["ins"]:
                operands.append(item["array"])
                in_specs.append(item["spec"])
            if stage.get("into") is not None:
                aliases[len(operands)] = len(out_shapes)
                operands.append(stage["into"])
                in_specs.append(anywhere)
            for shape in stage["outs"]:
                out_shapes.append(jax.ShapeDtypeStruct(shape, BF16))
                out_specs.append(anywhere if "into" in stage else near)
            scratch += stage.get("scratch", [])
        for array in (*after, *([] if self.last is None else [self.last])):
            operands.append(array)
            in_specs.append(pl.BlockSpec(memory_space=pl.ANY))
        n_in, n_out = len(operands), len(out_shapes)

        def kernel(*refs):
            ins, outs, tmp = list(refs[:n_in]), list(refs[n_in : n_in + n_out]), list(refs[n_in + n_out :])

            def take(refs, n):
                taken, refs[:n] = refs[:n], []
                return taken

            for stage in stages:
                given = take(ins, len(stage["ins"]))
                if stage.get("into") is not None:
                    take(ins, 1)
                stage["body"](given, take(outs, len(stage["outs"])), take(tmp, len(stage.get("scratch", []))))

        results = pl.pallas_call(
            kernel,
            out_shape=out_shapes,
            in_specs=in_specs,
            out_specs=out_specs,
            scratch_shapes=scratch,
            input_output_aliases=aliases,
            compiler_params=pltpu.CompilerParams(vmem_limit_bytes=vmem),
            cost_estimate=pl.CostEstimate(flops=1000, bytes_accessed=1000, transcendentals=0),
        )(*operands)
        self.last = results[0]
        grouped = []
        for stage in stages:
            grouped.append(results[: len(stage["outs"])])
            results = results[len(stage["outs"]) :]
        return grouped


def relu_sum(own, term, bias):
    return jnp.maximum(own + term.astype(F32) + bias, 0.0).astype(BF16)


def swap(value, axis, bit):
    return lax.ppermute(value, axis, [(i, i ^ 1 << bit) for i in range(lax.axis_size(axis))])


def pipelined(source_field, self_weight, cross_weight, level_bias, switch_weight, switch_bias):
    high_bit = lax.axis_size("src").bit_length() - 2
    pair_bit = high_bit - 1
    shots, blocks, width = source_field.shape
    half, piece = blocks // 2, width // 4
    packed = 128 // piece
    unit = shots // sum(UNITS)
    sizes = [unit * n for n in UNITS]
    starts = [sum(sizes[:t]) for t in range(len(sizes))]
    column, row = lax.axis_index("tgt") & 1, lax.axis_index("tgt") >> 1
    side = (lax.axis_index("src") >> pair_bit) & 1
    place = jnp.stack([side, row, column]).astype(jnp.int32)
    chain = Chain()

    cuts = (0, 2, 4)

    def pack(i):
        def body(ins, outs, tmp):
            self_w, cross_w, bias, where = ins
            (sent,) = outs
            other = (1 - where[0]) * half
            at = 0
            for weight, k in ((self_w, 2), (cross_w, 2), (self_w, 3), (cross_w, 3))[cuts[i] : cuts[i + 1]]:
                for b in range(half):
                    sent[at : at + width] = weight[k, other + b]
                    at += width
            if i == 0:
                return
            rows = []
            for row in [bias[2 + k, pl.ds(other + b, 1), :] for k in range(2) for b in range(half)]:
                for _ in range(3):
                    rounded = row.astype(BF16).astype(F32)
                    rows.append(rounded)
                    row = row - rounded
            rows += [jnp.zeros_like(rows[0])] * (-len(rows) % 16)
            sent[at:] = jnp.concatenate(rows).astype(BF16)

        extra = -(-6 * half // 16) * 16 if i == 1 else 0
        return dict(
            ins=[near(self_weight), near(cross_weight), near(level_bias), scalar(place)],
            outs=[((cuts[i + 1] - cuts[i]) * half * width + extra, width)],
            body=body,
        )

    def first(start, size):
        step = 128 if size % 128 == 0 else size

        def body(ins, outs, tmp):
            x, cross = ins
            rows, sent = outs
            (flat,) = tmp
            for at in range(0, size, step):
                for c in range(width // 128):
                    lanes = x[start + at : start + at + step, :, c * 128 : (c + 1) * 128]
                    flat[c] = lanes.astype(F32).reshape(step * blocks, 128)
                for b in range(blocks):
                    lanes = [flat[c, pl.ds(b, step, stride=blocks), :] for c in range(width // 128)]
                    field = jnp.concatenate(lanes, axis=1).astype(BF16)
                    rows[b, at : at + step] = field
                    sent[b, at : at + step] = dot(field, cross[0, b]).astype(BF16)

        return dict(
            ins=[near(source_field), near(cross_weight)],
            outs=[(blocks, size, width), (blocks, size, width)],
            scratch=[pltpu.VMEM((width // 128, step * blocks, 128), F32)],
            body=body,
        )

    def second(rows, term, start, size):
        def body(ins, outs, tmp):
            x, got, own_w, bias, cross = ins
            hidden, sent = outs
            rows = slice(start, start + size)
            for b in range(blocks):
                h = relu_sum(dot(x[b, rows], own_w[0, b]), got[b, rows], bias[0, b : b + 1, :])
                hidden[b] = h
                sent[b] = dot(h, cross[1, b]).astype(BF16)

        return dict(
            ins=[
                near(rows),
                near(term),
                near(self_weight),
                near(level_bias),
                near(cross_weight),
            ],
            outs=[(blocks, size, width), (blocks, size, width)],
            body=body,
        )

    def third(hidden, term, size):
        def body(ins, outs, tmp):
            x, got, own_w, bias, where = ins
            sent, kept = outs
            (pieces,) = tmp
            for b in range(0, blocks, packed):
                group = [
                    relu_sum(dot(x[c], own_w[1, c]), got[c], bias[1, c : c + 1, :]).astype(F32)
                    for c in range(b, b + packed)
                ]
                for j in range(4):
                    lanes = [h[:, j * piece : (j + 1) * piece] for h in group]
                    pieces[j, b // packed] = jnp.concatenate(lanes, axis=1).astype(BF16)
            for c in range(2):
                sent[c] = pieces[(1 - where[1]) * 2 + c]
                kept[c] = pieces[where[1] * 2 + c]

        shape = (2, blocks // packed, size, 128)
        return dict(
            ins=[near(hidden), near(term), near(self_weight), near(level_bias), scalar(place)],
            outs=[shape, shape],
            scratch=[pltpu.VMEM((4, *shape[1:]), BF16)],
            body=body,
        )

    def between(kept, came):
        def body(ins, outs, tmp):
            x, y, where = ins
            (sent,) = outs
            for i, pieces in enumerate((x, y)):
                sent[i] = pieces[1 - where[2]]

        return dict(
            ins=[near(kept), near(came), scalar(place)],
            outs=[kept.shape],
            body=body,
        )

    def fourth(kept, came, came_last, size):
        def body(ins, outs, tmp, message, at):
            x, y, z, weight, bias, where = ins
            (own,) = outs
            pieces, full = tmp
            row, column = where[1], where[2]
            pieces[row * 2 + column] = x[column]
            pieces[(1 - row) * 2 + column] = y[column]
            pieces[row * 2 + 1 - column] = z[0]
            pieces[(1 - row) * 2 + 1 - column] = z[1]
            for b in range(blocks):
                lane = b % packed * piece
                lanes = [pieces[g, b // packed].astype(F32)[:, lane : lane + piece] for g in range(4)]
                mixed = jnp.concatenate(lanes, axis=1).astype(BF16)
                full[b] = jnp.maximum(dot(mixed, weight[b]) + bias[b : b + 1, :], 0.0).astype(BF16)
            here = where[0]
            for b in range(half):
                message[at + b * size : at + (b + 1) * size] = full[(1 - here) * half + b]
                own[b] = full[here * half + b]

        return dict(
            ins=[near(kept), near(came), near(came_last), near(switch_weight), near(switch_bias), scalar(place)],
            outs=[(half, size, width)],
            scratch=[
                pltpu.VMEM((4, blocks // packed, size, 128), BF16),
                pltpu.VMEM((blocks, size, width), BF16),
            ],
            body=body,
        )

    def fifth(kept, came, start, size):
        def body(ins, outs, tmp, message, at):
            x, y = ins[:2]
            bias, where, self_w, cross_w = ins[2:6]
            v = ins[6:]

            def theirs(i, b):
                n = int(i >= cuts[1])
                at = ((i - cuts[n]) * half + b) * width
                return v[n][at : at + width]

            their_bias = v[1][(cuts[2] - cuts[1]) * half * width :].astype(F32)
            here = where[0] * half
            (own,) = outs
            for b in range(half):
                a, c = x[b], y[start + b * size : start + (b + 1) * size]
                for k in range(2):
                    bias_a = bias[2 + k, pl.ds(here + b, 1), :]
                    row = 3 * (k * half + b)
                    bias_c = their_bias[row : row + 1] + their_bias[row + 1 : row + 2] + their_bias[row + 2 : row + 3]
                    term_a = dot(a, cross_w[2 + k, here + b]).astype(BF16)
                    term_c = dot(c, theirs(2 * k + 1, b)).astype(BF16)
                    a, c = (
                        relu_sum(dot(a, self_w[2 + k, here + b]), term_c, bias_a),
                        relu_sum(dot(c, theirs(2 * k, b)), term_a, bias_c),
                    )
                own[b] = a
                message[at + b * size : at + (b + 1) * size] = c

        weights = [near(level_bias), scalar(place)]
        weights += [near(self_weight), near(cross_weight)]
        weights += [near(state["pack", i]) for i in range(2)]
        return dict(
            ins=[near(kept), near(came), *weights],
            outs=[(half, size, width)],
            body=body,
        )

    def exchange(stages):
        rows = [half * size for _, size in stages]
        parts = [stage for stage, _ in stages]

        def body(ins, outs, tmp):
            at = 0
            for n, stage in zip(rows, parts, strict=True):
                given = []
                for refs, kind in ((ins, "ins"), (outs, "outs"), (tmp, "scratch")):
                    many = len(stage.get(kind, []))
                    given.append(refs[:many])
                    del refs[:many]
                stage["body"](*given, message=outs[-1], at=at)
                at += n

        join = lambda kind: [item for stage in parts for item in stage.get(kind, [])]
        return dict(ins=join("ins"), outs=[*join("outs"), (sum(rows), width)], scratch=join("scratch"), body=body)

    def sixth(start, own, came, first_row, out, size):
        def body(ins, outs, tmp):
            x, y, where = ins
            (result,) = outs
            flat, laid, sem = tmp
            here = where[0]
            for b in range(half):
                mine = x[b].astype(F32)
                other = y[first_row + b * size : first_row + (b + 1) * size].astype(F32)
                for c in range(width // 128):
                    lanes = slice(c * 128, (c + 1) * 128)
                    flat[c, pl.ds(here * half + b, size, stride=blocks), :] = mine[:, lanes]
                    flat[c, pl.ds((1 - here) * half + b, size, stride=blocks), :] = other[:, lanes]
            for c in range(width // 128):
                lanes = slice(c * 128, (c + 1) * 128)
                laid[:, :, lanes] = flat[c].reshape(size, blocks, 128).astype(BF16)
            copy = pltpu.make_async_copy(laid, result.at[pl.ds(start, size)], sem)
            copy.start()
            copy.wait()

        return dict(
            ins=[near(own), near(came), scalar(place)],
            into=out,
            outs=[(shots, blocks, width)],
            scratch=[
                pltpu.VMEM((width // 128, size * blocks, 128), F32),
                pltpu.VMEM((size, blocks, width), BF16),
                pltpu.SemaphoreType.DMA,
            ],
            body=body,
        )

    count = len(sizes)
    early = sum(sizes[:EARLY])
    state = {}
    out = None

    def run(*names, after=(), vmem=VMEM_BYTES):
        nonlocal out
        inside = lambda t: 0 <= t < count
        names = [(name, tuple(one for one in t if inside(one[1]))) if name == "swap" else (name, t) for name, t in names]
        names = [(name, t) for name, t in names if (t if name == "swap" else name == "pack" or inside(t))]
        stages = []
        for name, t in names:
            size = None if name == "swap" else sizes[t]
            if name == "first":
                stages.append(first(0, early) if t == 0 else first(early, shots - early))
            elif name == "second":
                late = starts[t] >= early
                stages.append(second(*state["first", int(late)], starts[t] - late * early, size))
            elif name == "third":
                stages.append(third(*state.pop(("second", t)), size))
            elif name == "between":
                stages.append(between(*state["third", t]))
            elif name == "pack":
                stages.append(pack(t))
            elif name == "swap":
                pairs = []
                for kind, u in t:
                    if kind == "fourth":
                        stage = fourth(*state.pop(("third", u)), state.pop(("between", u)), sizes[u])
                    else:
                        stage = fifth(*state.pop(("fourth", u)), sizes[u])
                    pairs.append((stage, sizes[u]))
                stages.append(exchange(pairs))
            else:
                stages.append(sixth(starts[t], *state.pop(("fifth", t)), out, size))
        for (name, t), got in zip(names, chain(*stages, after=after, vmem=vmem), strict=True):
            if name == "first":
                state[name, t] = got[0], swap(got[1], "src", 0)
            elif name == "second":
                state[name, t] = got[0], swap(got[1], "src", high_bit)
            elif name == "third":
                state[name, t] = got[1], swap(got[0], "tgt", 1)
            elif name == "between":
                state[name, t] = swap(got[0], "tgt", 0)
            elif name == "pack":
                state[name, t] = swap(got[0], "src", pair_bit)
            elif name == "swap":
                came, at = swap(got[-1], "src", pair_bit), 0
                state["came"] = came
                for (kind, u), own in zip(t, got[:-1], strict=True):
                    state[kind, u] = own, came, at
                    at += half * sizes[u]
            else:
                (out,) = got

    run(("pack", 0))
    run(("first", 0))
    run(("second", 0))
    run(("second", 1))
    run(("second", 2))
    run(("second", 3))
    run(("pack", 1))
    run(("third", 0))
    run(("third", 1), after=(state["pack", 0],))
    run(("between", 0))
    run(("between", 1))
    run(("third", 2))
    run(("swap", (("fourth", 0), ("fourth", 1))))
    run(("second", 4), ("between", 2), after=(state["pack", 1],))
    run(("third", 3), ("second", 5))
    for t in range(3, count):
        if t > 3:
            run(("third", t), ("second", t + 2))
        last = state["came"]
        run(("swap", (("fourth", t - 1), ("fifth", t - 3))))
        run(("between", t), after=(last,))
        run(("sixth", t - 5))
    run(("swap", (("fourth", count - 1),)))
    run(("sixth", count - 5))
    run(("swap", (("fifth", count - 3),)))
    run(("swap", (("fifth", count - 2),)))
    run(("sixth", count - 4))
    run(("swap", (("fifth", count - 1),)))
    run(("sixth", count - 3))
    run(("sixth", count - 2))
    run(("sixth", count - 1))
    return out


def level_step(field, self_w, cross_w, bias, bit):
    own = jnp.einsum("sbi,bio->sbo", field, self_w, preferred_element_type=F32)
    term = jnp.einsum("sbi,bio->sbo", field, cross_w, preferred_element_type=F32).astype(BF16)
    return relu_sum(own, swap(term, "src", bit), bias[None])


def stepwise(source_field, self_weight, cross_weight, level_bias, switch_weight, switch_bias):
    high_bit = lax.axis_size("src").bit_length() - 2
    bits = [0, high_bit, high_bit - 1, 1]
    field = source_field
    for k in range(4):
        field = level_step(field, self_weight[k], cross_weight[k], level_bias[k], bits[k])
        if k == 1:
            mixed = lax.all_to_all(field, "tgt", split_axis=2, concat_axis=2, tiled=True)
            product = jnp.einsum("sbi,bio->sbo", mixed, switch_weight, preferred_element_type=F32)
            field = jnp.maximum(product + switch_bias[None], 0.0).astype(BF16)
    return field


def solution(mesh):
    placed = (
        P(None, ("src", "tgt"), None),
        P(None, ("src", "tgt"), None, None),
        P(None, ("src", "tgt"), None, None),
        P(None, ("src", "tgt"), None),
        P(("src", "tgt"), None, None),
        P(("src", "tgt"), None),
    )
    same_pairs = mesh.shape["src"].bit_length() - 3 == 1
    per_device = pipelined if same_pairs and mesh.shape["tgt"] == 4 else stepwise
    return jax.shard_map(
        per_device,
        mesh=mesh,
        in_specs=placed,
        out_specs=P(None, ("src", "tgt"), None),
        check_vma=False,
    )
```

```python
import jax
import jax.numpy as jnp
from jax import lax
from jax.experimental import pallas as pl
from jax.experimental.pallas import tpu as pltpu
from jax.sharding import PartitionSpec as P

UNITS = (2, 2, 2, 2, 2, 2, 2, 2)
EARLY = 8
F32, BF16 = jnp.float32, jnp.bfloat16
VMEM_BYTES = 5 << 20


def dot(a, b):
    return jnp.dot(a, b, preferred_element_type=F32)


def near(array):
    return dict(array=array, spec=pl.BlockSpec(memory_space=pltpu.VMEM))


def far(array):
    return dict(array=array, spec=pl.BlockSpec(memory_space=pltpu.HBM))


def scalar(array):
    return dict(array=array, spec=pl.BlockSpec(memory_space=pltpu.SMEM))


class Chain:
    def __init__(self):
        self.last = None

    def __call__(self, *stages, after=(), vmem=VMEM_BYTES):
        if not stages:
            return []
        anywhere = pl.BlockSpec(memory_space=pltpu.HBM)
        near = pl.BlockSpec(memory_space=pltpu.VMEM)
        operands, in_specs, out_shapes, out_specs, scratch, aliases = [], [], [], [], [], {}
        for stage in stages:
            for item in stage["ins"]:
                operands.append(item["array"])
                in_specs.append(item["spec"])
            if stage.get("into") is not None:
                aliases[len(operands)] = len(out_shapes)
                operands.append(stage["into"])
                in_specs.append(anywhere)
            for shape in stage["outs"]:
                out_shapes.append(jax.ShapeDtypeStruct(shape, BF16))
                out_specs.append(anywhere if "into" in stage else near)
            scratch += stage.get("scratch", [])
        for array in (*after, *([] if self.last is None else [self.last])):
            operands.append(array)
            in_specs.append(pl.BlockSpec(memory_space=pl.ANY))
        n_in, n_out = len(operands), len(out_shapes)

        def kernel(*refs):
            ins, outs, tmp = list(refs[:n_in]), list(refs[n_in : n_in + n_out]), list(refs[n_in + n_out :])

            def take(refs, n):
                taken, refs[:n] = refs[:n], []
                return taken

            for stage in stages:
                given = take(ins, len(stage["ins"]))
                if stage.get("into") is not None:
                    take(ins, 1)
                stage["body"](given, take(outs, len(stage["outs"])), take(tmp, len(stage.get("scratch", []))))

        results = pl.pallas_call(
            kernel,
            out_shape=out_shapes,
            in_specs=in_specs,
            out_specs=out_specs,
            scratch_shapes=scratch,
            input_output_aliases=aliases,
            compiler_params=pltpu.CompilerParams(vmem_limit_bytes=vmem),
            cost_estimate=pl.CostEstimate(flops=1000, bytes_accessed=1000, transcendentals=0),
        )(*operands)
        self.last = results[0]
        grouped = []
        for stage in stages:
            grouped.append(results[: len(stage["outs"])])
            results = results[len(stage["outs"]) :]
        return grouped


def relu_sum(own, term, bias):
    return jnp.maximum(own + term.astype(F32) + bias, 0.0).astype(BF16)


def swap(value, axis, bit):
    return lax.ppermute(value, axis, [(i, i ^ 1 << bit) for i in range(lax.axis_size(axis))])


def pipelined(source_field, self_weight, cross_weight, level_bias, switch_weight, switch_bias):
    high_bit = lax.axis_size("src").bit_length() - 2
    pair_bit = high_bit - 1
    shots, blocks, width = source_field.shape
    half, piece = blocks // 2, width // 4
    packed = 128 // piece
    unit = shots // sum(UNITS)
    sizes = [unit * n for n in UNITS]
    starts = [sum(sizes[:t]) for t in range(len(sizes))]
    column, row = lax.axis_index("tgt") & 1, lax.axis_index("tgt") >> 1
    side = (lax.axis_index("src") >> pair_bit) & 1
    place = jnp.stack([side, row, column]).astype(jnp.int32)
    chain = Chain()

    cuts = (0, 2, 4)

    def pack(i):
        def body(ins, outs, tmp):
            self_w, cross_w, bias, where = ins
            (sent,) = outs
            other = (1 - where[0]) * half
            at = 0
            for weight, k in ((self_w, 2), (cross_w, 2), (self_w, 3), (cross_w, 3))[cuts[i] : cuts[i + 1]]:
                for b in range(half):
                    sent[at : at + width] = weight[k, other + b]
                    at += width
            if i == 0:
                return
            rows = []
            for row in [bias[2 + k, pl.ds(other + b, 1), :] for k in range(2) for b in range(half)]:
                for _ in range(3):
                    rounded = row.astype(BF16).astype(F32)
                    rows.append(rounded)
                    row = row - rounded
            rows += [jnp.zeros_like(rows[0])] * (-len(rows) % 16)
            sent[at:] = jnp.concatenate(rows).astype(BF16)

        extra = -(-6 * half // 16) * 16 if i == 1 else 0
        return dict(
            ins=[near(self_weight), near(cross_weight), near(level_bias), scalar(place)],
            outs=[((cuts[i + 1] - cuts[i]) * half * width + extra, width)],
            body=body,
        )

    def first(start, size):
        step = 128 if size % 128 == 0 else size

        def body(ins, outs, tmp):
            x, cross = ins
            rows, sent = outs
            (flat,) = tmp
            for at in range(0, size, step):
                for c in range(width // 128):
                    lanes = x[start + at : start + at + step, :, c * 128 : (c + 1) * 128]
                    flat[c] = lanes.astype(F32).reshape(step * blocks, 128)
                for b in range(blocks):
                    lanes = [flat[c, pl.ds(b, step, stride=blocks), :] for c in range(width // 128)]
                    field = jnp.concatenate(lanes, axis=1).astype(BF16)
                    rows[b, at : at + step] = field
                    sent[b, at : at + step] = dot(field, cross[0, b]).astype(BF16)

        return dict(
            ins=[near(source_field), near(cross_weight)],
            outs=[(blocks, size, width), (blocks, size, width)],
            scratch=[pltpu.VMEM((width // 128, step * blocks, 128), F32)],
            body=body,
        )

    def second(rows, term, start, size):
        def body(ins, outs, tmp):
            x, got, own_w, bias, cross = ins
            hidden, sent = outs
            rows = slice(start, start + size)
            for b in range(blocks):
                h = relu_sum(dot(x[b, rows], own_w[0, b]), got[b, rows], bias[0, b : b + 1, :])
                hidden[b] = h
                sent[b] = dot(h, cross[1, b]).astype(BF16)

        return dict(
            ins=[
                near(rows),
                near(term),
                near(self_weight),
                near(level_bias),
                near(cross_weight),
            ],
            outs=[(blocks, size, width), (blocks, size, width)],
            body=body,
        )

    def third(hidden, term, size):
        def body(ins, outs, tmp):
            x, got, own_w, bias, where = ins
            sent, kept = outs
            (pieces,) = tmp
            for b in range(0, blocks, packed):
                group = [
                    relu_sum(dot(x[c], own_w[1, c]), got[c], bias[1, c : c + 1, :]).astype(F32)
                    for c in range(b, b + packed)
                ]
                for j in range(4):
                    lanes = [h[:, j * piece : (j + 1) * piece] for h in group]
                    pieces[j, b // packed] = jnp.concatenate(lanes, axis=1).astype(BF16)
            for c in range(2):
                sent[c] = pieces[(1 - where[1]) * 2 + c]
                kept[c] = pieces[where[1] * 2 + c]

        shape = (2, blocks // packed, size, 128)
        return dict(
            ins=[near(hidden), near(term), near(self_weight), near(level_bias), scalar(place)],
            outs=[shape, shape],
            scratch=[pltpu.VMEM((4, *shape[1:]), BF16)],
            body=body,
        )

    def between(kept, came):
        def body(ins, outs, tmp):
            x, y, where = ins
            (sent,) = outs
            for i, pieces in enumerate((x, y)):
                sent[i] = pieces[1 - where[2]]

        return dict(
            ins=[near(kept), near(came), scalar(place)],
            outs=[kept.shape],
            body=body,
        )

    def fourth(kept, came, came_last, size):
        def body(ins, outs, tmp, message, at):
            x, y, z, weight, bias, where = ins
            (own,) = outs
            pieces, full = tmp
            row, column = where[1], where[2]
            pieces[row * 2 + column] = x[column]
            pieces[(1 - row) * 2 + column] = y[column]
            pieces[row * 2 + 1 - column] = z[0]
            pieces[(1 - row) * 2 + 1 - column] = z[1]
            for b in range(blocks):
                lane = b % packed * piece
                lanes = [pieces[g, b // packed].astype(F32)[:, lane : lane + piece] for g in range(4)]
                mixed = jnp.concatenate(lanes, axis=1).astype(BF16)
                full[b] = jnp.maximum(dot(mixed, weight[b]) + bias[b : b + 1, :], 0.0).astype(BF16)
            here = where[0]
            for b in range(half):
                message[at + b * size : at + (b + 1) * size] = full[(1 - here) * half + b]
                own[b] = full[here * half + b]

        return dict(
            ins=[near(kept), near(came), near(came_last), near(switch_weight), near(switch_bias), scalar(place)],
            outs=[(half, size, width)],
            scratch=[
                pltpu.VMEM((4, blocks // packed, size, 128), BF16),
                pltpu.VMEM((blocks, size, width), BF16),
            ],
            body=body,
        )

    def fifth(kept, came, start, size):
        def body(ins, outs, tmp, message, at):
            x, y = ins[:2]
            bias, where, self_w, cross_w = ins[2:6]
            v = ins[6:]

            def theirs(i, b):
                n = int(i >= cuts[1])
                at = ((i - cuts[n]) * half + b) * width
                return v[n][at : at + width]

            their_bias = v[1][(cuts[2] - cuts[1]) * half * width :].astype(F32)
            here = where[0] * half
            (own,) = outs
            for b in range(half):
                a, c = x[b], y[start + b * size : start + (b + 1) * size]
                for k in range(2):
                    bias_a = bias[2 + k, pl.ds(here + b, 1), :]
                    row = 3 * (k * half + b)
                    bias_c = their_bias[row : row + 1] + their_bias[row + 1 : row + 2] + their_bias[row + 2 : row + 3]
                    term_a = dot(a, cross_w[2 + k, here + b]).astype(BF16)
                    term_c = dot(c, theirs(2 * k + 1, b)).astype(BF16)
                    a, c = (
                        relu_sum(dot(a, self_w[2 + k, here + b]), term_c, bias_a),
                        relu_sum(dot(c, theirs(2 * k, b)), term_a, bias_c),
                    )
                own[b] = a
                message[at + b * size : at + (b + 1) * size] = c

        weights = [near(level_bias), scalar(place)]
        weights += [near(self_weight), near(cross_weight)]
        weights += [near(state["pack", i]) for i in range(2)]
        return dict(
            ins=[near(kept), near(came), *weights],
            outs=[(half, size, width)],
            body=body,
        )

    def exchange(stages):
        rows = [half * size for _, size in stages]
        parts = [stage for stage, _ in stages]

        def body(ins, outs, tmp):
            at = 0
            for n, stage in zip(rows, parts, strict=True):
                given = []
                for refs, kind in ((ins, "ins"), (outs, "outs"), (tmp, "scratch")):
                    many = len(stage.get(kind, []))
                    given.append(refs[:many])
                    del refs[:many]
                stage["body"](*given, message=outs[-1], at=at)
                at += n

        join = lambda kind: [item for stage in parts for item in stage.get(kind, [])]
        return dict(ins=join("ins"), outs=[*join("outs"), (sum(rows), width)], scratch=join("scratch"), body=body)

    def sixth(start, own, came, first_row, out, size):
        def body(ins, outs, tmp):
            x, y, where = ins
            (result,) = outs
            flat, laid, sem = tmp
            here = where[0]
            for b in range(half):
                mine = x[b].astype(F32)
                other = y[first_row + b * size : first_row + (b + 1) * size].astype(F32)
                for c in range(width // 128):
                    lanes = slice(c * 128, (c + 1) * 128)
                    flat[c, pl.ds(here * half + b, size, stride=blocks), :] = mine[:, lanes]
                    flat[c, pl.ds((1 - here) * half + b, size, stride=blocks), :] = other[:, lanes]
            for c in range(width // 128):
                lanes = slice(c * 128, (c + 1) * 128)
                laid[:, :, lanes] = flat[c].reshape(size, blocks, 128).astype(BF16)
            copy = pltpu.make_async_copy(laid, result.at[pl.ds(start, size)], sem)
            copy.start()
            copy.wait()

        return dict(
            ins=[near(own), near(came), scalar(place)],
            into=out,
            outs=[(shots, blocks, width)],
            scratch=[
                pltpu.VMEM((width // 128, size * blocks, 128), F32),
                pltpu.VMEM((size, blocks, width), BF16),
                pltpu.SemaphoreType.DMA,
            ],
            body=body,
        )

    count = len(sizes)
    early = sum(sizes[:EARLY])
    state = {}
    out = None

    def run(*names, after=(), vmem=VMEM_BYTES):
        nonlocal out
        inside = lambda t: 0 <= t < count
        names = [(name, tuple(one for one in t if inside(one[1]))) if name == "swap" else (name, t) for name, t in names]
        names = [(name, t) for name, t in names if (t if name == "swap" else name == "pack" or inside(t))]
        stages = []
        for name, t in names:
            size = None if name == "swap" else sizes[t]
            if name == "first":
                stages.append(first(0, early) if t == 0 else first(early, shots - early))
            elif name == "second":
                late = starts[t] >= early
                stages.append(second(*state["first", int(late)], starts[t] - late * early, size))
            elif name == "third":
                stages.append(third(*state.pop(("second", t)), size))
            elif name == "between":
                stages.append(between(*state["third", t]))
            elif name == "pack":
                stages.append(pack(t))
            elif name == "swap":
                pairs = []
                for kind, u in t:
                    if kind == "fourth":
                        stage = fourth(*state.pop(("third", u)), state.pop(("between", u)), sizes[u])
                    else:
                        stage = fifth(*state.pop(("fourth", u)), sizes[u])
                    pairs.append((stage, sizes[u]))
                stages.append(exchange(pairs))
            else:
                stages.append(sixth(starts[t], *state.pop(("fifth", t)), out, size))
        for (name, t), got in zip(names, chain(*stages, after=after, vmem=vmem), strict=True):
            if name == "first":
                state[name, t] = got[0], swap(got[1], "src", 0)
            elif name == "second":
                state[name, t] = got[0], swap(got[1], "src", high_bit)
            elif name == "third":
                state[name, t] = got[1], swap(got[0], "tgt", 1)
            elif name == "between":
                state[name, t] = swap(got[0], "tgt", 0)
            elif name == "pack":
                state[name, t] = swap(got[0], "src", pair_bit)
            elif name == "swap":
                came, at = swap(got[-1], "src", pair_bit), 0
                state["came"] = came
                for (kind, u), own in zip(t, got[:-1], strict=True):
                    state[kind, u] = own, came, at
                    at += half * sizes[u]
            else:
                (out,) = got

    run(("pack", 0))
    run(("first", 0))
    run(("second", 0))
    run(("second", 1))
    run(("second", 2))
    run(("second", 3))
    run(("pack", 1))
    run(("third", 0))
    run(("third", 1), after=(state["pack", 0],))
    run(("between", 0))
    run(("between", 1))
    run(("third", 2))
    run(("swap", (("fourth", 0), ("fourth", 1))))
    run(("second", 4), ("second", 5), ("between", 2), after=(state["pack", 1],))
    run(("third", 3), ("second", 6))
    for t in range(3, count):
        if t > 3:
            run(("third", t), ("second", t + 3))
        last = state["came"]
        run(("swap", (("fourth", t - 1), ("fifth", t - 3))))
        run(("between", t), after=(last,))
        run(("sixth", t - 5))
    run(("swap", (("fourth", count - 1),)))
    run(("sixth", count - 5))
    run(("swap", (("fifth", count - 3),)))
    run(("swap", (("fifth", count - 2),)))
    run(("sixth", count - 4))
    run(("swap", (("fifth", count - 1),)))
    run(("sixth", count - 3))
    run(("sixth", count - 2))
    run(("sixth", count - 1))
    return out


def level_step(field, self_w, cross_w, bias, bit):
    own = jnp.einsum("sbi,bio->sbo", field, self_w, preferred_element_type=F32)
    term = jnp.einsum("sbi,bio->sbo", field, cross_w, preferred_element_type=F32).astype(BF16)
    return relu_sum(own, swap(term, "src", bit), bias[None])


def stepwise(source_field, self_weight, cross_weight, level_bias, switch_weight, switch_bias):
    high_bit = lax.axis_size("src").bit_length() - 2
    bits = [0, high_bit, high_bit - 1, 1]
    field = source_field
    for k in range(4):
        field = level_step(field, self_weight[k], cross_weight[k], level_bias[k], bits[k])
        if k == 1:
            mixed = lax.all_to_all(field, "tgt", split_axis=2, concat_axis=2, tiled=True)
            product = jnp.einsum("sbi,bio->sbo", mixed, switch_weight, preferred_element_type=F32)
            field = jnp.maximum(product + switch_bias[None], 0.0).astype(BF16)
    return field


def solution(mesh):
    placed = (
        P(None, ("src", "tgt"), None),
        P(None, ("src", "tgt"), None, None),
        P(None, ("src", "tgt"), None, None),
        P(None, ("src", "tgt"), None),
        P(("src", "tgt"), None, None),
        P(("src", "tgt"), None),
    )
    same_pairs = mesh.shape["src"].bit_length() - 3 == 1
    per_device = pipelined if same_pairs and mesh.shape["tgt"] == 4 else stepwise
    return jax.shard_map(
        per_device,
        mesh=mesh,
        in_specs=placed,
        out_specs=P(None, ("src", "tgt"), None),
        check_vma=False,
    )
```
